128 devices in a mesh: ctx: 16 (over y, z), head: 8 (over x, core).
Axes of the slice: x: 4, y: 4, z: 4, core: 2. Of those that a mesh axis runs over, the one named last changes fastest.
Arguments:
- query: bfloat16 [32768, 3072], P(('ctx', 'head')), may hold values from -150 to 150
- key_in: bfloat16 [32768, 3072], P(('ctx', 'head')), may hold values from -6 to 6
- value: bfloat16 [32768, 3072], P(('ctx', 'head')), may hold values from -6 to 6
- out_grad: bfloat16 [32768, 3072], P(('ctx', 'head')), may hold values from -6 to 6
- segment: int32 [32768], replicated, may hold values from 0 to 2, never falling along the last dimension, each value on 1 to 20480 neighbouring positions
- kv_list: int32 [256, 6], replicated, may hold values from 0 to 255, as said below
Outputs:
- attended: bfloat16 [32768, 3072], P(('ctx', 'head'))
- grad_query: bfloat16 [32768, 3072], P(('ctx', 'head'))
- grad_key: bfloat16 [32768, 3072], P(('ctx', 'head'))
- grad_value: bfloat16 [32768, 3072], P(('ctx', 'head'))
The draws below stay inside these ranges and needn't reach their ends.
Inputs may be any that keep to these rules, and one draw needn't show every extreme that they name: `kv_list`: row t lists 6 different tiles and starts with t. Take the aligned ranges of 16 tiles (k*16 to k*16 + 15): every row lists exactly 3 tiles outside its own range, and the rows of one range list together exactly 2 different tiles of every other range.
All inputs are finite; a program needn't handle non-finite values.
Results may differ from the reference program's by a relative error of at most 0.04.
Values may be sent and summed in bfloat16 or wider, within the bound.
A program may use at most 192 MiB of HBM per device.

```python
import math
import jax
import jax.numpy as jnp
import numpy as np
from jax import lax

HEADS = 24
HEAD_DIM = 128
D = 3072
TILE = 128
LIST = 6
REMOTE = 3
CAP = 2
TPD = 16
TOKENS = 32768
QTILES = 256


def shared_keys(key):
    base = jax.random.normal(jax.random.fold_in(key, 900), (TOKENS, D), jnp.float32)
    base = jnp.clip(base, -6.0, 6.0)
    return base


def draw_key_in(key, part):
    base = shared_keys(key)
    return base.astype(jnp.bfloat16)


def draw_query(key, part):
    key = jax.random.fold_in(key, 3)
    fresh = jnp.clip(jax.random.normal(key, (TOKENS, D), jnp.float32), -6.0, 6.0)
    return fresh.astype(jnp.bfloat16)


def draw_kv_list(key, part):
    key = jax.random.fold_in(key, 17)
    key_own, key_pool, key_local = jax.random.split(key, 3)
    ranges = QTILES // TPD
    pool_size = (ranges - 1) * CAP
    raw_pick = jax.random.randint(key_own, (ranges, ranges, TPD), 0, 1 << 20) * TPD + jnp.arange(TPD)
    picked = jnp.argsort(raw_pick, axis=2)[:, :, :CAP]
    owners = (jnp.arange(ranges)[:, None] + jnp.arange(1, ranges)[None, :]) % ranges
    chosen = jnp.take_along_axis(picked, owners[:, :, None], axis=1)
    pool = (owners[:, :, None] * TPD + chosen).reshape(ranges, pool_size)
    raw_order = jax.random.randint(key_pool, (ranges, pool_size), 0, 1 << 20) * pool_size + jnp.arange(pool_size)
    pool = jnp.take_along_axis(pool, jnp.argsort(raw_order, axis=1), axis=1)
    spots = (jnp.arange(TPD)[:, None] * REMOTE + jnp.arange(REMOTE)[None, :]) % pool_size
    remote = pool[:, spots]
    nlocal = LIST - 1 - REMOTE
    raw_local = jax.random.randint(key_local, (ranges, TPD, TPD - 1), 0, 1 << 20) * (TPD - 1) + jnp.arange(TPD - 1)
    offsets = jnp.argsort(raw_local, axis=2)[:, :, :nlocal] + 1
    local = (jnp.arange(TPD)[None, :, None] + offsets) % TPD + jnp.arange(ranges)[:, None, None] * TPD
    first = jnp.arange(QTILES).reshape(ranges, TPD, 1)
    listed = jnp.concatenate([first, remote, local], axis=2).reshape(QTILES, LIST)
    return listed.astype(jnp.int32)


def shard_levels(stream_key, extent, pieces, smallest, top_value):
    gain, own = 1.0, jax.random.fold_in(stream_key, 6)
    for dim, shards_of in pieces:
        steps = jnp.exp(jax.random.uniform(jax.random.fold_in(own, dim), (shards_of,), jnp.float32, smallest / len(pieces), top_value / len(pieces)))
        gain = gain * jnp.repeat(steps, extent[dim] // shards_of).reshape([-1 if axis == dim else 1 for axis in range(len(extent))])
    return gain


def profile(amount, total, most, slope):
    portions = [(1 << 20) // math.isqrt(grade ** slope) + 1 for grade in range(2, amount + 1)]
    spare, holding = total - most - (amount - 1), [1] * (amount - 1)
    while spare > 0:
        free = [i for i in range(amount - 1) if holding[i] < most]
        whole, budget = sum([portions[i] for i in free]), spare
        for i in free:
            extra = min(most - holding[i], max(1, budget * portions[i] // whole), spare)
            holding[i] = holding[i] + extra
            spare = spare - extra
    return np.array([most] + holding)


def ragged(own_key, count, total, most, skew):
    if count == 2:
        one = jax.random.randint(own_key, (), max(1, total - most), min(most, total - 1) + 1)
        return jnp.stack([one, total - one])
    tallies = jnp.asarray(profile(count, total, most, skew), jnp.int32)
    couples = (count - 1) // 2
    giver, sink = tallies[1:1 + 2 * couples:2], tallies[2:2 + 2 * couples:2]
    margin = jnp.minimum(giver - 1, most - sink)
    passed = jax.random.randint(jax.random.fold_in(own_key, 1), (couples,), 0, 1 << 20) % (margin + 1)
    tallies = tallies.at[1:1 + 2 * couples:2].set(giver - passed).at[2:2 + 2 * couples:2].set(sink + passed)
    return tallies[jax.random.permutation(jax.random.fold_in(own_key, 2), count)]


def noise(own_key, dims, deviation, limit, cuts=(), held_as=jnp.bfloat16):
    entries = jax.random.normal(own_key, dims, jnp.float32) * deviation
    if len(cuts) > 0:
        entries = shard_levels(own_key, dims, cuts, -0.22, 0.18) * entries
    return jnp.clip(entries, min=-limit, max=limit).astype(held_as)


def setup_inputs(seed: int = 0) -> dict:
    key_list = jax.random.split(jax.random.key(seed), 7)
    return {
        "query": draw_query(jax.random.fold_in(key_list[6], 71), 0),
        "key_in": draw_key_in(jax.random.fold_in(key_list[6], 71), 0),
        "value": noise(key_list[2], (TOKENS, D), 1.0, 6.0, ((0, 128),)),
        "out_grad": noise(key_list[3], (TOKENS, D), 1.0, 6.0, ((0, 128),)),
        "segment": jnp.searchsorted(jnp.cumsum(ragged(key_list[4], 3, TOKENS, TOKENS * 5 // 8, 0)), jnp.arange(TOKENS), side="right").astype(jnp.int32),
        "kv_list": draw_kv_list(jax.random.fold_in(key_list[6], 71), 0),
    }


masked_score = -1.0e30


def reference(query, key_in, value, out_grad, segment, kv_list):
    scale = HEAD_DIM ** -0.5
    query_tiles = query.reshape(QTILES, TILE, HEADS, HEAD_DIM)
    key_tiles = key_in.reshape(QTILES, TILE, HEADS, HEAD_DIM)
    value_tiles = value.reshape(QTILES, TILE, HEADS, HEAD_DIM)
    grad_tiles = out_grad.reshape(QTILES, TILE, HEADS, HEAD_DIM)
    seg_tiles = segment.reshape(QTILES, TILE)

    def visit(carry, tile_id):
        key_grads, value_grads = carry
        listed = kv_list[tile_id].astype(jnp.int32)
        queries = query_tiles[tile_id].astype(jnp.float32)
        keys = key_tiles[listed].reshape(LIST * TILE, HEADS, HEAD_DIM).astype(jnp.float32)
        values = value_tiles[listed].reshape(LIST * TILE, HEADS, HEAD_DIM).astype(jnp.float32)
        grads = grad_tiles[tile_id].astype(jnp.float32)
        scores = jnp.einsum("qhd,khd->hqk", queries, keys) * scale
        allowed = seg_tiles[tile_id][:, None] == seg_tiles[listed].reshape(-1)[None, :]
        scores = jnp.where(allowed[None], scores, masked_score)
        top = jnp.max(scores, axis=-1, keepdims=True)
        expd = jnp.exp(scores - top)
        probs = expd / jnp.sum(expd, axis=-1, keepdims=True)
        probs_low = lax.optimization_barrier(probs.astype(jnp.bfloat16)).astype(jnp.float32)
        attended = lax.optimization_barrier(jnp.einsum("hqk,khd->qhd", probs_low, values).astype(jnp.bfloat16))
        grad_probs = jnp.einsum("qhd,khd->hqk", grads, values)
        row_dot = jnp.sum(grads * attended.astype(jnp.float32), axis=-1)
        grad_scores = probs * (grad_probs - jnp.transpose(row_dot)[:, :, None])
        grad_scores = lax.optimization_barrier(grad_scores.astype(jnp.bfloat16)).astype(jnp.float32)
        grad_query = (jnp.einsum("hqk,khd->qhd", grad_scores, keys) * scale).astype(jnp.bfloat16)
        tile_keys = jnp.einsum("hqk,qhd->khd", grad_scores, queries) * scale
        tile_values = jnp.einsum("hqk,qhd->khd", probs_low, grads)
        key_grads = key_grads.at[listed].add(tile_keys.reshape(LIST, TILE, HEADS, HEAD_DIM))
        value_grads = value_grads.at[listed].add(tile_values.reshape(LIST, TILE, HEADS, HEAD_DIM))
        return (key_grads, value_grads), (attended, grad_query)

    zeros = jnp.zeros((QTILES, TILE, HEADS, HEAD_DIM), jnp.float32)
    (key_grads, value_grads), (attended, grad_query) = lax.scan(visit, (zeros, zeros), jnp.arange(QTILES, dtype=jnp.int32))
    return (attended.reshape(TOKENS, D), grad_query.reshape(TOKENS, D),
            key_grads.astype(jnp.bfloat16).reshape(TOKENS, D), value_grads.astype(jnp.bfloat16).reshape(TOKENS, D))
```

```python
import functools

import jax
import jax.numpy as jnp
from jax import lax
from jax.experimental import pallas as pl
from jax.experimental.pallas import tpu as pltpu
from jax.sharding import PartitionSpec as P

HEAD_DIM = 128
TILE = 128
LIST = 6
CAP = 2
TPD = 16
NCTX = 16
NHEAD = 8
HPD = 3
NREM = (NCTX - 1) * CAP
SLOTS = TPD + NREM
ROWS = TPD * LIST
HALF = ROWS // 2
MASKED = -1e30
SCALE = HEAD_DIM**-0.5
LOG2E = 1.4426950408889634
MESH = pl.DeviceIdType.MESH

OFFSETS = (
    (0, 1), (0, 3), (1, 0), (3, 0), (0, 2), (2, 0), (1, 1), (3, 3),
    (1, 3), (3, 1), (1, 2), (3, 2), (2, 1), (2, 3), (2, 2),
)

T_SLOT = 0
T_TILE = T_SLOT + ROWS
T_WANT = T_TILE + ROWS
T_LPERM = T_WANT + NREM
T_LSAME = T_LPERM + HALF
T_LLAST = T_LSAME + HALF
T_RPERM = T_LLAST + TPD
T_RSAME = T_RPERM + HALF
T_RLAST = T_RSAME + HALF
T_BPERM = T_RLAST + NREM
T_BSAME = T_BPERM + NREM
T_BLAST = T_BSAME + NREM
T_EDGE = T_BLAST + TPD
T_SIZE = T_EDGE + 2


def relative(y, z, other):
    return ((other // 4 - y) % 4) * 4 + (other % 4 - z) % 4


def sorted_runs(keys, valid, count):
    n = keys.shape[0]
    index = jnp.arange(n, dtype=jnp.int32)
    full = jnp.where(valid, keys * n + index, 1 << 20)
    place = jnp.sum((full[None, :] < full[:, None]).astype(jnp.int32), axis=1)
    places = jnp.arange(count, dtype=jnp.int32)
    hit = (place[None, :] == places[:, None]) & valid[None, :]
    perm = jnp.sum(jnp.where(hit, index[None, :], 0), axis=1)
    key_at = jnp.sum(jnp.where(hit, keys[None, :], 0), axis=1)
    before = jnp.concatenate([jnp.full((1,), -1, jnp.int32), key_at[:-1]])
    return perm, (key_at == before).astype(jnp.int32)


def tables(segment, kv_list):
    me = lax.axis_index("ctx")
    y, z = me // 4, me % 4
    entries = kv_list.reshape(NCTX, ROWS)
    owner, within = entries // TPD, entries % TPD
    mine = lax.dynamic_index_in_dim(entries, me, 0, keepdims=False)
    own, inside = mine // TPD, mine % TPD
    same_owner = own[None, :] == own[:, None]
    low = jnp.min(jnp.where(same_owner, inside[None, :], TPD), axis=1)
    rank = (inside != low).astype(jnp.int32)
    local = own == me
    slot = jnp.where(local, inside, TPD + CAP * (relative(y, z, own) - 1) + rank)
    step = jnp.arange(1, NCTX, dtype=jnp.int32)
    requester = ((y + step // 4) % 4) * 4 + (z + step % 4) % 4
    asked = owner == me
    first = jnp.min(jnp.where(asked, within, TPD), axis=1)
    second = jnp.max(jnp.where(asked, within, -1), axis=1)
    pick = requester[:, None] == jnp.arange(NCTX, dtype=jnp.int32)[None, :]
    want = jnp.stack(
        [
            jnp.sum(jnp.where(pick, first[None, :], 0), axis=1),
            jnp.sum(jnp.where(pick, second[None, :], 0), axis=1),
        ],
        axis=1,
    ).reshape(NREM)
    tiles = jnp.arange(TPD, dtype=jnp.int32)
    rems = jnp.arange(NREM, dtype=jnp.int32)
    l_perm, l_same = sorted_runs(slot, local, HALF)
    l_last = jnp.sum((local[None, :] & (slot[None, :] <= tiles[:, None])).astype(jnp.int32), axis=1) - 1
    r_perm, r_same = sorted_runs(slot, ~local, HALF)
    r_last = jnp.sum((~local[None, :] & (slot[None, :] - TPD <= rems[:, None])).astype(jnp.int32), axis=1) - 1
    b_perm, b_same = sorted_runs(want, jnp.ones((NREM,), bool), NREM)
    upto = jnp.sum((want[None, :] <= tiles[:, None]).astype(jnp.int32), axis=1)
    b_last = jnp.where(jnp.any(want[None, :] == tiles[:, None], axis=1), upto, 0)
    edges = jnp.stack([jnp.sum((segment < 1).astype(jnp.int32)), jnp.sum((segment < 2).astype(jnp.int32))])
    return jnp.concatenate(
        [slot, mine, want, l_perm, l_same, l_last, r_perm, r_same, r_last, b_perm, b_same, b_last, edges]
    ).astype(jnp.int32)


def dot_nt(a, b):
    return lax.dot_general(a, b, (((1,), (1,)), ((), ())), preferred_element_type=jnp.float32)


def dot_nn(a, b):
    return lax.dot_general(a, b, (((1,), (0,)), ((), ())), preferred_element_type=jnp.float32)


def dot_tn(a, b):
    return lax.dot_general(a, b, (((0,), (0,)), ((), ())), preferred_element_type=jnp.float32)


def attend(tab, me, q, g, k_all, v_all, o_out, dq_out, c_key, c_value):
    edge1, edge2 = tab[T_EDGE], tab[T_EDGE + 1]
    end = NCTX * TPD * TILE

    def one(i, carry):
        query, grad = q[i], g[i]
        slots = [tab[T_SLOT + i * LIST + j] for j in range(LIST)]
        keys = jnp.concatenate([k_all[s] for s in slots], axis=0)
        values = jnp.concatenate([v_all[s] for s in slots], axis=0)
        scores = dot_nt(query, keys) * (SCALE * LOG2E)
        at = (me * TPD + i) * TILE + lax.broadcasted_iota(jnp.int32, (TILE, TILE), 0)
        start = jnp.where(at >= edge2, edge2, jnp.where(at >= edge1, edge1, 0))
        stop = jnp.where(at >= edge2, end, jnp.where(at >= edge1, edge2, edge1))
        lane = lax.broadcasted_iota(jnp.int32, (TILE, TILE), 1)
        parts = []
        for j in range(LIST):
            key_at = tab[T_TILE + i * LIST + j] * TILE + lane
            allowed = (key_at >= start) & (key_at < stop)
            parts.append(jnp.where(allowed, scores[:, j * TILE : (j + 1) * TILE], MASKED))
        scores = jnp.concatenate(parts, axis=1)
        top = jnp.max(scores, axis=1, keepdims=True)
        expd = jnp.exp2(scores - top)
        probs = expd * (1.0 / jnp.sum(expd, axis=1, keepdims=True))
        low = probs.astype(jnp.bfloat16)
        attended = dot_nn(low, values).astype(jnp.bfloat16)
        o_out[i] = attended
        grad_probs = dot_nt(grad, values)
        row_dot = jnp.sum(grad.astype(jnp.float32) * attended.astype(jnp.float32), axis=1, keepdims=True)
        grad_scores = (probs * (grad_probs - row_dot)).astype(jnp.bfloat16)
        dq_out[i] = (dot_nn(grad_scores, keys) * SCALE).astype(jnp.bfloat16)
        key_part = (dot_tn(grad_scores, query) * SCALE).astype(jnp.bfloat16)
        value_part = dot_tn(low, grad).astype(jnp.bfloat16)
        c_key[pl.ds(i * LIST, LIST)] = key_part.reshape(LIST, TILE, HEAD_DIM)
        c_value[pl.ds(i * LIST, LIST)] = value_part.reshape(LIST, TILE, HEAD_DIM)
        return carry

    lax.fori_loop(0, TPD, one, 0)


def run_sums(tab, perm, same, count, parts, out, shift=0):
    def one(p, total):
        total = jnp.where(tab[same + p] == 1, total, 0.0) + parts[tab[perm + p]].astype(jnp.float32)
        out[p + shift] = total.astype(out.dtype)
        return total

    lax.fori_loop(0, count, one, jnp.zeros((TILE, HEAD_DIM), jnp.float32))


def wait_bytes(ref, sem):
    pltpu.make_async_copy(ref, ref, sem).wait()


def kernel(tab, q_in, k_in, v_in, g_in, o_out, dq_out, dk_out, dv_out, *scratch):
    it = iter(scratch)

    def take(n):
        return [next(it) for _ in range(n)]

    q_loc, g_loc, k_loc, v_loc = take(HPD), take(HPD), take(HPD), take(HPD)
    k_all, v_all = take(HPD), take(HPD)
    k_stage, v_stage = take(HPD), take(HPD)
    k_back, v_back = take(HPD), take(HPD)
    o_stage, dq_stage, dk_stage, dv_stage = take(HPD), take(HPD), take(HPD), take(HPD)
    k_sum, v_sum = take(HPD), take(HPD)
    c_key, c_value, run_local, run_remote, run_back = take(5)
    x_send, x_recv, c_send, c_recv, b_send, b_recv, y_send, y_recv = take(8)

    me, head = lax.axis_index("ctx"), lax.axis_index("head")
    y, z = me // 4, me % 4

    barrier = pltpu.get_barrier_semaphore()
    for d in range(1, NHEAD):
        pl.semaphore_signal(barrier, inc=1, device_id=(me, (head + d) % NHEAD), device_id_type=MESH)
    for dy, dz in OFFSETS:
        peer = ((y + dy) % 4) * 4 + (z + dz) % 4
        pl.semaphore_signal(barrier, inc=1, device_id=(peer, head), device_id_type=MESH)
    pl.semaphore_wait(barrier, NHEAD - 1 + NCTX - 1)

    def columns(owner, h):
        return pl.ds(pl.multiple_of((owner * HPD + h) * HEAD_DIM, HEAD_DIM), HEAD_DIM)

    def pair(index):
        return pl.ds(2 * index, 2)

    def send_in(a, h):
        src, dst = (q_in, k_in, v_in, g_in)[a], (q_loc, k_loc, v_loc, g_loc)[a][h]
        for d in range(1, NHEAD):
            peer = (head + d) % NHEAD
            pltpu.make_async_remote_copy(
                src_ref=src.at[:, :, columns(peer, h)],
                dst_ref=dst.at[pair(head)],
                send_sem=x_send.at[a],
                recv_sem=x_recv.at[a, h],
                device_id=(me, peer),
                device_id_type=MESH,
            ).start()
        pltpu.make_async_copy(src.at[:, :, columns(head, h)], dst.at[pair(head)], x_recv.at[a, h]).start()

    def wait_in(a, h):
        wait_bytes((q_loc, k_loc, v_loc, g_loc)[a][h], x_recv.at[a, h])

    def send_out(a, h):
        src, dst = (o_stage, dq_stage, dk_stage, dv_stage)[a][h], (o_out, dq_out, dk_out, dv_out)[a]
        for d in range(1, NHEAD):
            peer = (head + d) % NHEAD
            pltpu.make_async_remote_copy(
                src_ref=src.at[pair(peer)],
                dst_ref=dst.at[:, :, columns(head, h)],
                send_sem=y_send.at[a],
                recv_sem=y_recv.at[a],
                device_id=(me, peer),
                device_id_type=MESH,
            ).start()
        pltpu.make_async_copy(src.at[pair(head)], dst.at[:, :, columns(head, h)], y_recv.at[a]).start()

    def send_ctx(stage, landing, base, send_sem, recv_sem):
        for dy, dz in OFFSETS:
            there = dy * 4 + dz - 1
            here = ((-dy) % 4) * 4 + (-dz) % 4 - 1
            peer = ((y + dy) % 4) * 4 + (z + dz) % 4
            pltpu.make_async_remote_copy(
                src_ref=stage.at[pl.ds(CAP * there, CAP)],
                dst_ref=landing.at[pl.ds(base + CAP * here, CAP)],
                send_sem=send_sem,
                recv_sem=recv_sem,
                device_id=(peer, head),
                device_id_type=MESH,
            ).start()

    Q, K, V, G = 0, 1, 2, 3
    for a, h in ((K, 0), (V, 0), (K, 1), (V, 1), (Q, 0), (G, 0), (K, 2), (V, 2), (Q, 1), (G, 1), (Q, 2), (G, 2)):
        send_in(a, h)

    def forward_tiles(a, h):
        wait_in(a, h)
        s = a - K
        local, stage, everything = (k_loc, v_loc)[s][h], (k_stage, v_stage)[s][h], (k_all, v_all)[s][h]

        def pack(p, carry):
            stage[p] = local[tab[T_WANT + p]]
            return carry

        lax.fori_loop(0, NREM, pack, 0)
        send_ctx(stage, everything, TPD, c_send.at[s, h], c_recv.at[s, h])

        def keep(p, carry):
            everything[p] = local[p]
            return carry

        lax.fori_loop(0, TPD, keep, 0)

    for h in range(HPD):
        forward_tiles(K, h)
        forward_tiles(V, h)

    for h in range(HPD):
        wait_in(Q, h)
        wait_in(G, h)
        for s in range(2):
            wait_bytes((k_all, v_all)[s][h].at[pl.ds(TPD, NREM)], c_recv.at[s, h])
        attend(tab, me, q_loc[h], g_loc[h], k_all[h], v_all[h], o_stage[h], dq_stage[h], c_key, c_value)
        send_out(0, h)
        send_out(1, h)
        for s in range(2):
            parts, stage, landing = (c_key, c_value)[s], (k_stage, v_stage)[s][h], (k_back, v_back)[s][h]
            run_sums(tab, T_RPERM, T_RSAME, HALF, parts, run_remote)
            wait_bytes(stage, c_send.at[s, h])

            def fill(p, carry, stage=stage):
                stage[p] = run_remote[tab[T_RLAST + p]]
                return carry

            lax.fori_loop(0, NREM, fill, 0)
            send_ctx(stage, landing, 0, b_send.at[s, h], b_recv.at[s, h])
        for s in range(2):
            parts, sums = (c_key, c_value)[s], (k_sum, v_sum)[s][h]
            run_sums(tab, T_LPERM, T_LSAME, HALF, parts, run_local)

            def settle(p, carry, sums=sums):
                sums[p] = run_local[tab[T_LLAST + p]]
                return carry

            lax.fori_loop(0, TPD, settle, 0)

    run_back[0] = jnp.zeros((TILE, HEAD_DIM), jnp.float32)
    for h in range(HPD):
        for s in range(2):
            back, sums, stage = (k_back, v_back)[s][h], (k_sum, v_sum)[s][h], (dk_stage, dv_stage)[s][h]
            wait_bytes(back, b_recv.at[s, h])
            run_sums(tab, T_BPERM, T_BSAME, NREM, back, run_back, shift=1)

            def finish(p, carry, sums=sums, stage=stage):
                stage[p] = (sums[p] + run_back[tab[T_BLAST + p]]).astype(jnp.bfloat16)
                return carry

            lax.fori_loop(0, TPD, finish, 0)
            send_out(2 + s, h)

    sent = CAP * (NHEAD - 1) * HPD
    for a in range(4):
        wait_bytes(k_all[0].at[pl.ds(0, sent)], x_send.at[a])
        wait_bytes(k_all[0].at[pl.ds(0, sent)], y_send.at[a])
        wait_bytes((o_out, dq_out, dk_out, dv_out)[a], y_recv.at[a])
    for s in range(2):
        for h in range(HPD):
            wait_bytes((k_stage, v_stage)[s][h], b_send.at[s, h])


def body(query, key_in, value, out_grad, segment, kv_list):
    tab = tables(segment, kv_list)
    tokens, width = query.shape
    shape = (tokens // TILE, TILE, width)
    bf16, f32 = jnp.bfloat16, jnp.float32

    def vmem(n, dtype=bf16):
        return pltpu.VMEM((n, TILE, HEAD_DIM), dtype)

    scratch = (
        [vmem(TPD)] * (4 * HPD)
        + [vmem(SLOTS)] * (2 * HPD)
        + [vmem(NREM)] * (2 * HPD)
        + [vmem(NREM)] * (2 * HPD)
        + [vmem(TPD)] * (4 * HPD)
        + [vmem(TPD, f32)] * (2 * HPD)
        + [vmem(ROWS), vmem(ROWS), vmem(HALF, f32), vmem(HALF), vmem(NREM + 1, f32)]
        + [
            pltpu.SemaphoreType.DMA((4,)),
            pltpu.SemaphoreType.DMA((4, HPD)),
            pltpu.SemaphoreType.DMA((2, HPD)),
            pltpu.SemaphoreType.DMA((2, HPD)),
            pltpu.SemaphoreType.DMA((2, HPD)),
            pltpu.SemaphoreType.DMA((2, HPD)),
            pltpu.SemaphoreType.DMA((4,)),
            pltpu.SemaphoreType.DMA((4,)),
        ]
    )
    outs = pl.pallas_call(
        kernel,
        out_shape=[jax.ShapeDtypeStruct(shape, bf16)] * 4,
        in_specs=[pl.BlockSpec(memory_space=pltpu.SMEM)] + [pl.BlockSpec(memory_space=pl.ANY)] * 4,
        out_specs=[pl.BlockSpec(memory_space=pl.ANY)] * 4,
        scratch_shapes=scratch,
        compiler_params=pltpu.CompilerParams(
            collective_id=0, has_side_effects=True, vmem_limit_bytes=60 * 1024 * 1024
        ),
        cost_estimate=pl.CostEstimate(flops=7_250_000_000, bytes_accessed=12_600_000, transcendentals=4_718_592),
        name="sparse_attention",
    )(tab, *(a.reshape(shape) for a in (query, key_in, value, out_grad)))
    return tuple(o.reshape(tokens, width) for o in outs)


def solution(mesh):
    tokens = P(("ctx", "head"), None)
    return jax.shard_map(
        body,
        mesh=mesh,
        in_specs=(tokens, tokens, tokens, tokens, P(), P()),
        out_specs=(tokens, tokens, tokens, tokens),
        check_vma=False,
    )
```

```python
import jax
import jax.numpy as jnp
from jax import lax
from jax.experimental import pallas as pl
from jax.experimental.pallas import tpu as pltpu
from jax.sharding import PartitionSpec as P

HEAD_DIM = 128
TILE = 128
LIST = 6
CAP = 2
TPD = 16
NCTX = 16
NHEAD = 8
HPD = 3
NREM = (NCTX - 1) * CAP
SLOTS = TPD + NREM
ROWS = TPD * LIST
HALF = ROWS // 2
MASKED = -1e30
SCALE = HEAD_DIM**-0.5
LOG2E = 1.4426950408889634
MESH = pl.DeviceIdType.MESH

OFFSETS = (
    (0, 1), (2, 3), (0, 3), (2, 1), (1, 0), (3, 2), (3, 0), (1, 2),
    (0, 2), (2, 0), (2, 2), (1, 1), (3, 3), (1, 3), (3, 1),
)

WHOLE = ((0, TILE),)
HALVES = ((0, TILE // 2), (TILE // 2, TILE // 2))
PARTS_IN = {(s, h): WHOLE for s in range(2) for h in range(HPD)} | {(0, 0): HALVES}
PARTS_BACK = {(s, h): WHOLE for s in range(2) for h in range(HPD)} | {(1, HPD - 1): HALVES}
MOST_PARTS = 2

T_SLOT, T_TILE, T_WANT = 0, 1, 2
T_LPERM, T_LSAME, T_LLAST = 3, 4, 5
T_RPERM, T_RSAME, T_RLAST = 6, 7, 8
T_BPERM, T_BSAME, T_BLAST = 9, 10, 11
T_EDGE = 12
T_ROWS = 16


def relative(y, z, other):
    return (((other >> 2) - y) & 3) * 4 + (((other & 3) - z) & 3)


def build_tables(me, kv, seg, table):
    y, z = me // 4, me % 4
    big = 1 << 20
    sub = lax.broadcasted_iota(jnp.int32, (TILE, TILE), 0)
    lane = lax.broadcasted_iota(jnp.int32, (TILE, TILE), 1)
    at = lax.broadcasted_iota(jnp.int32, (TILE, 1), 0)
    eye = sub == lane

    def to_row(col):
        return jnp.sum(jnp.where(eye, col, 0), axis=0, keepdims=True)

    def count(mask):
        return jnp.sum(jnp.where(mask, 1, 0), axis=0, keepdims=True)

    def runs(key_c, key_r, valid_c, valid_r):
        full_c = jnp.where(valid_c, key_c * TILE + at, big)
        full_r = jnp.where(valid_r, key_r * TILE + lane, big)
        place = jnp.sum(jnp.where(full_r < full_c, 1, 0), axis=1, keepdims=True)
        hit = (place == lane) & valid_c
        after = (place + 1 == lane) & valid_c
        perm = jnp.sum(jnp.where(hit, sub, 0), axis=0, keepdims=True)
        key = jnp.sum(jnp.where(hit, key_c + 1, 0), axis=0, keepdims=True)
        before = jnp.sum(jnp.where(after, key_c + 1, 0), axis=0, keepdims=True)
        return perm, jnp.where(key == before, 1, 0)

    wide = lax.broadcasted_iota(jnp.int32, (TILE, NCTX * TPD), 1)
    rows = [kv[j : j + 1, :] for j in range(LIST)]
    low = jnp.full((1, NCTX * TPD), TPD, jnp.int32)
    high = jnp.full((1, NCTX * TPD), -1, jnp.int32)
    for row in rows:
        asked = (row >> 4) == me
        low = jnp.where(asked, jnp.minimum(low, row & 15), low)
        high = jnp.where(asked, jnp.maximum(high, row & 15), high)
    step = (at >> 1) + 1
    asker = ((y + (step >> 2)) & 3) * 4 + ((z + (step & 3)) & 3)
    group = (wide >> 4) == asker
    first = jnp.min(jnp.where(group, low, TPD), axis=1, keepdims=True)
    second = jnp.max(jnp.where(group, high, -1), axis=1, keepdims=True)
    want_c = jnp.clip(jnp.where((at & 1) == 0, first, second), 0, TPD - 1)
    want_r = to_row(want_c)
    mine_c = jnp.zeros((TILE, 1), jnp.int32)
    for j in range(LIST):
        here = (wide == me * TPD + (at & 15)) & ((at >> 4) == j)
        mine_c = mine_c + jnp.sum(jnp.where(here, rows[j], 0), axis=1, keepdims=True)
    mine_r = to_row(mine_c)
    own_c, own_r = mine_c >> 4, mine_r >> 4
    in_c, in_r = mine_c & 15, mine_r & 15
    real_c, real_r = at < ROWS, lane < ROWS
    lowest = jnp.min(jnp.where((own_c == own_r) & real_r, in_r, TPD), axis=1, keepdims=True)
    rank = jnp.where(in_c != lowest, 1, 0)
    slot_c = jnp.where(own_c == me, in_c, TPD + CAP * (relative(y, z, own_c) - 1) + rank)
    slot_r = to_row(slot_c)
    local_c, local_r = (own_c == me) & real_c, (own_r == me) & real_r
    other_c, other_r = (own_c != me) & real_c, (own_r != me) & real_r
    l_perm, l_same = runs(slot_c, slot_r, local_c, local_r)
    r_perm, r_same = runs(slot_c, slot_r, other_c, other_r)
    asked_c, asked_r = at < NREM, lane < NREM
    b_perm, b_same = runs(want_c, want_r, asked_c, asked_r)
    upto = count((want_c <= lane) & asked_c)
    b_last = jnp.where(count((want_c == lane) & asked_c) > 0, upto, 0)
    edges = []
    for value in (1, 2):
        per_lane = jnp.sum(jnp.where(seg[...] < value, 1, 0), axis=0, keepdims=True)
        edges.append(jnp.sum(per_lane, axis=1, keepdims=True))
    lane_r = lax.broadcasted_iota(jnp.int32, (1, TILE), 1)
    found = {
        T_SLOT: slot_r,
        T_TILE: mine_r,
        T_WANT: want_r,
        T_LPERM: l_perm,
        T_LSAME: l_same,
        T_LLAST: jnp.clip(count((slot_c <= lane) & local_c) - 1, 0, HALF - 1),
        T_RPERM: r_perm,
        T_RSAME: r_same,
        T_RLAST: jnp.clip(count((slot_c - TPD <= lane) & other_c) - 1, 0, HALF - 1),
        T_BPERM: b_perm,
        T_BSAME: b_same,
        T_BLAST: b_last,
        T_EDGE: jnp.where(lane_r == 0, edges[0], edges[1]),
    }
    none = jnp.zeros((1, TILE), jnp.int32)
    table[...] = jnp.concatenate([found.get(r, none) for r in range(T_ROWS)], axis=0)


def dot_nt(a, b):
    return lax.dot_general(a, b, (((1,), (1,)), ((), ())), preferred_element_type=jnp.float32)


def dot_nn(a, b):
    return lax.dot_general(a, b, (((1,), (0,)), ((), ())), preferred_element_type=jnp.float32)


def dot_tn(a, b):
    return lax.dot_general(a, b, (((0,), (0,)), ((), ())), preferred_element_type=jnp.float32)


def attend(tab, me, q, g, k_all, v_all, o_out, dq_out, c_key, c_value):
    edge1, edge2 = tab[T_EDGE, 0], tab[T_EDGE, 1]
    end = NCTX * TPD * TILE

    def one(i, carry):
        query, grad = q[i], g[i]
        slots = [tab[T_SLOT, j * TPD + i] for j in range(LIST)]
        keys = jnp.concatenate([k_all[s] for s in slots], axis=0)
        values = jnp.concatenate([v_all[s] for s in slots], axis=0)
        scores = dot_nt(query, keys) * (SCALE * LOG2E)
        at = (me * TPD + i) * TILE + lax.broadcasted_iota(jnp.int32, (TILE, TILE), 0)
        start = jnp.where(at >= edge2, edge2, jnp.where(at >= edge1, edge1, 0))
        stop = jnp.where(at >= edge2, end, jnp.where(at >= edge1, edge2, edge1))
        lane = lax.broadcasted_iota(jnp.int32, (TILE, TILE), 1)
        parts = []
        for j in range(LIST):
            key_at = tab[T_TILE, j * TPD + i] * TILE + lane
            allowed = (key_at >= start) & (key_at < stop)
            parts.append(jnp.where(allowed, scores[:, j * TILE : (j + 1) * TILE], MASKED))
        scores = jnp.concatenate(parts, axis=1)
        top = jnp.max(scores, axis=1, keepdims=True)
        expd = jnp.exp2(scores - top)
        probs = expd * (1.0 / jnp.sum(expd, axis=1, keepdims=True))
        low = probs.astype(jnp.bfloat16)
        attended = dot_nn(low, values).astype(jnp.bfloat16)
        o_out[i] = attended
        grad_probs = dot_nt(grad, values)
        row_dot = jnp.sum(grad.astype(jnp.float32) * attended.astype(jnp.float32), axis=1, keepdims=True)
        grad_scores = (probs * (grad_probs - row_dot)).astype(jnp.bfloat16)
        dq_out[i] = (dot_nn(grad_scores, keys) * SCALE).astype(jnp.bfloat16)
        key_part = (dot_tn(grad_scores, query) * SCALE).astype(jnp.bfloat16)
        value_part = dot_tn(low, grad).astype(jnp.bfloat16)
        for j in range(LIST):
            c_key[j * TPD + i] = key_part[j * TILE : (j + 1) * TILE]
            c_value[j * TPD + i] = value_part[j * TILE : (j + 1) * TILE]
        return carry

    lax.fori_loop(0, TPD, one, 0)


def run_sums(tab, perm, same, count, parts, out, shift=0, rows=TILE):
    def one(p, total):
        total = jnp.where(tab[same, p] == 1, total, 0.0) + parts[tab[perm, p]].astype(jnp.float32)
        out[p + shift, pl.ds(0, rows)] = total.astype(out.dtype)
        return total

    lax.fori_loop(0, count, one, jnp.zeros((rows, HEAD_DIM), jnp.float32))


def wait_bytes(ref, sem):
    pltpu.make_async_copy(ref, ref, sem).wait()


def kernel(q_in, k_in, v_in, g_in, seg_in, kv_in, o_out, dq_out, dk_out, dv_out, *scratch):
    it = iter(scratch)

    def take(n):
        return [next(it) for _ in range(n)]

    def take_parts(parts):
        return {(s, h): take(len(parts[s, h])) for s in range(2) for h in range(HPD)}

    q_loc, g_loc = take(HPD), take(HPD)
    kv_loc, kv_back = take_parts(PARTS_IN), take_parts(PARTS_BACK)
    k_all, v_all = take(HPD), take(HPD)
    k_stage, v_stage = take(HPD), take(HPD)
    o_stage, dq_stage, dk_stage, dv_stage = take(HPD), take(HPD), take(HPD), take(HPD)
    k_sum, v_sum = take(HPD), take(HPD)
    c_key, c_value, run_local, run_remote, run_back = take(5)
    kv, seg, table, tab, t_sem = take(5)
    x_send, x_recv, c_send, c_recv, b_send, b_recv, y_send, y_recv = take(8)

    me, head = lax.axis_index("ctx"), lax.axis_index("head")
    y, z = me // 4, me % 4

    fetches = [pltpu.make_async_copy(kv_in, kv, t_sem.at[0]), pltpu.make_async_copy(seg_in, seg, t_sem.at[1])]
    for fetch in fetches:
        fetch.start()

    barrier = pltpu.get_barrier_semaphore()
    for d in range(1, NHEAD):
        pl.semaphore_signal(barrier, inc=1, device_id=(me, (head + d) % NHEAD), device_id_type=MESH)
    for dy, dz in OFFSETS:
        peer = ((y + dy) % 4) * 4 + (z + dz) % 4
        pl.semaphore_signal(barrier, inc=1, device_id=(peer, head), device_id_type=MESH)
    pl.semaphore_wait(barrier, NHEAD - 1 + NCTX - 1)

    def columns(owner, h):
        return pl.ds(pl.multiple_of((owner * HPD + h) * HEAD_DIM, HEAD_DIM), HEAD_DIM)

    def pair(index):
        return pl.ds(2 * index, 2)

    def send_in(src, dst, rows, h, send_sem, recv_sem):
        for d in range(1, NHEAD):
            peer = (head + d) % NHEAD
            pltpu.make_async_remote_copy(
                src_ref=src.at[:, pl.ds(*rows), columns(peer, h)],
                dst_ref=dst.at[pair(head)],
                send_sem=send_sem,
                recv_sem=recv_sem,
                device_id=(me, peer),
                device_id_type=MESH,
            ).start()
        pltpu.make_async_copy(src.at[:, pl.ds(*rows), columns(head, h)], dst.at[pair(head)], recv_sem).start()

    def send_kv(s, h):
        for n, rows in enumerate(PARTS_IN[s, h]):
            send_in((k_in, v_in)[s], kv_loc[s, h][n], rows, h, x_send.at[2 + s], x_recv.at[2 + s, h, n])

    def send_qg(h):
        send_in(q_in, q_loc[h], WHOLE[0], h, x_send.at[0], x_recv.at[0, h, 0])
        send_in(g_in, g_loc[h], WHOLE[0], h, x_send.at[1], x_recv.at[1, h, 0])

    def send_out(a, h, rows):
        src, dst = (o_stage, dq_stage, dk_stage, dv_stage)[a][h], (o_out, dq_out, dk_out, dv_out)[a]
        for d in range(1, NHEAD):
            peer = (head + d) % NHEAD
            pltpu.make_async_remote_copy(
                src_ref=src.at[pair(peer), pl.ds(*rows)],
                dst_ref=dst.at[:, pl.ds(*rows), columns(head, h)],
                send_sem=y_send.at[a],
                recv_sem=y_recv.at[a],
                device_id=(me, peer),
                device_id_type=MESH,
            ).start()
        pltpu.make_async_copy(
            src.at[pair(head), pl.ds(*rows)], dst.at[:, pl.ds(*rows), columns(head, h)], y_recv.at[a]
        ).start()

    def send_ctx(stage, landing, base, rows, landing_rows, send_sem, recv_sem):
        for dy, dz in OFFSETS:
            there = dy * 4 + dz - 1
            here = ((-dy) % 4) * 4 + (-dz) % 4 - 1
            peer = ((y + dy) % 4) * 4 + (z + dz) % 4
            pltpu.make_async_remote_copy(
                src_ref=stage.at[pl.ds(CAP * there, CAP), pl.ds(*rows)],
                dst_ref=landing.at[pl.ds(base + CAP * here, CAP), pl.ds(*landing_rows)],
                send_sem=send_sem,
                recv_sem=recv_sem,
                device_id=(peer, head),
                device_id_type=MESH,
            ).start()

    def forward_tiles(s, h):
        stage, everything = (k_stage, v_stage)[s][h], (k_all, v_all)[s][h]
        for n, rows in enumerate(PARTS_IN[s, h]):
            local = kv_loc[s, h][n]
            wait_bytes(local, x_recv.at[2 + s, h, n])

            def pack(p, carry, local=local, rows=rows):
                stage[p, pl.ds(*rows)] = local[tab[T_WANT, p]]
                return carry

            lax.fori_loop(0, NREM, pack, 0)
            send_ctx(stage, everything, TPD, rows, rows, c_send.at[s, h, n], c_recv.at[s, h, n])

            def keep(p, carry, local=local, rows=rows):
                everything[p, pl.ds(*rows)] = local[p]
                return carry

            lax.fori_loop(0, TPD, keep, 0)

    send_kv(0, 0)
    send_kv(1, 0)
    for fetch in fetches:
        fetch.wait()
    build_tables(me, kv, seg, table)
    to_scalar = pltpu.make_async_copy(table, tab, t_sem.at[2])
    to_scalar.start()
    to_scalar.wait()
    send_kv(0, 1)
    forward_tiles(0, 0)
    send_kv(1, 1)
    send_qg(0)
    forward_tiles(1, 0)
    send_kv(0, 2)
    send_kv(1, 2)
    forward_tiles(0, 1)
    send_qg(1)
    forward_tiles(1, 1)
    send_qg(2)
    forward_tiles(0, 2)
    forward_tiles(1, 2)

    for h in range(HPD):
        wait_bytes(q_loc[h], x_recv.at[0, h, 0])
        wait_bytes(g_loc[h], x_recv.at[1, h, 0])
        for s in range(2):
            for n, rows in enumerate(PARTS_IN[s, h]):
                wait_bytes((k_all, v_all)[s][h].at[pl.ds(TPD, NREM), pl.ds(*rows)], c_recv.at[s, h, n])
        attend(tab, me, q_loc[h], g_loc[h], k_all[h], v_all[h], o_stage[h], dq_stage[h], c_key, c_value)
        send_out(0, h, WHOLE[0])
        send_out(1, h, WHOLE[0])
        for s in range(2):
            stage = (k_stage, v_stage)[s][h]
            run_sums(tab, T_RPERM, T_RSAME, HALF, (c_key, c_value)[s], run_remote)
            for n, rows in enumerate(PARTS_IN[s, h]):
                wait_bytes(stage.at[:, pl.ds(*rows)], c_send.at[s, h, n])

            def fill(p, carry, stage=stage):
                stage[p] = run_remote[tab[T_RLAST, p]]
                return carry

            lax.fori_loop(0, NREM, fill, 0)
            for n, rows in enumerate(PARTS_BACK[s, h]):
                landing = kv_back[s, h][n]
                send_ctx(stage, landing, 0, rows, (0, rows[1]), b_send.at[s, h, n], b_recv.at[s, h, n])
        for s in range(2):
            sums = (k_sum, v_sum)[s][h]
            run_sums(tab, T_LPERM, T_LSAME, HALF, (c_key, c_value)[s], run_local)

            def settle(p, carry, sums=sums):
                sums[p] = run_local[tab[T_LLAST, p]]
                return carry

            lax.fori_loop(0, TPD, settle, 0)

    run_back[0] = jnp.zeros((TILE, HEAD_DIM), jnp.float32)
    for h in range(HPD):
        for s in range(2):
            sums, stage = (k_sum, v_sum)[s][h], (dk_stage, dv_stage)[s][h]
            for n, rows in enumerate(PARTS_BACK[s, h]):
                back = kv_back[s, h][n]
                wait_bytes(back, b_recv.at[s, h, n])
                run_sums(tab, T_BPERM, T_BSAME, NREM, back, run_back, shift=1, rows=rows[1])

                def finish(p, carry, sums=sums, stage=stage, rows=rows):
                    total = sums[p, pl.ds(*rows)] + run_back[tab[T_BLAST, p], pl.ds(0, rows[1])]
                    stage[p, pl.ds(*rows)] = total.astype(jnp.bfloat16)
                    return carry

                lax.fori_loop(0, TPD, finish, 0)
                send_out(2 + s, h, rows)

    sent = CAP * (NHEAD - 1) * HPD
    for a in range(4):
        wait_bytes(k_all[0].at[pl.ds(0, sent)], x_send.at[a])
        wait_bytes(k_all[0].at[pl.ds(0, sent)], y_send.at[a])
        wait_bytes((o_out, dq_out, dk_out, dv_out)[a], y_recv.at[a])
    for s in range(2):
        for h in range(HPD):
            for n, rows in enumerate(PARTS_BACK[s, h]):
                wait_bytes((k_stage, v_stage)[s][h].at[:, pl.ds(*rows)], b_send.at[s, h, n])


def hand_over(*refs):
    source, result, (held, come, go) = refs[:4], refs[4:8], refs[8:]
    pieces = [(a, p) for a in range(4) for p in range(2)]
    coming = [pltpu.make_async_copy(source[a].at[p], held.at[a, p], come.at[a, p]) for a, p in pieces]
    going = [pltpu.make_async_copy(held.at[a, p], result[a].at[p], go.at[a, p]) for a, p in pieces]
    for copy in coming:
        copy.start()
    for copy, onward in zip(coming, going):
        copy.wait()
        onward.start()
    for onward in going:
        onward.wait()


def body(query, key_in, value, out_grad, segment, kv_list):
    tokens, width = query.shape
    shape = (tokens // TILE, TILE, width)
    bf16, f32 = jnp.bfloat16, jnp.float32

    def vmem(n, dtype=bf16, rows=TILE):
        return pltpu.VMEM((n, rows, HEAD_DIM), dtype)

    def vmem_parts(n, parts):
        return [vmem(n, rows=rows) for s in range(2) for h in range(HPD) for _, rows in parts[s, h]]

    scratch = (
        [vmem(TPD)] * (2 * HPD)
        + vmem_parts(TPD, PARTS_IN)
        + vmem_parts(NREM, PARTS_BACK)
        + [vmem(SLOTS)] * (2 * HPD)
        + [vmem(NREM)] * (2 * HPD)
        + [vmem(TPD)] * (4 * HPD)
        + [vmem(TPD, f32)] * (2 * HPD)
        + [vmem(ROWS), vmem(ROWS), vmem(HALF, f32), vmem(HALF), vmem(NREM + 1, f32)]
        + [
            pltpu.VMEM((LIST, NCTX * TPD), jnp.int32),
            pltpu.VMEM((NCTX * TPD, TILE), jnp.int32),
            pltpu.VMEM((T_ROWS, TILE), jnp.int32),
            pltpu.SMEM((T_ROWS, TILE), jnp.int32),
            pltpu.SemaphoreType.DMA((3,)),
            pltpu.SemaphoreType.DMA((4,)),
            pltpu.SemaphoreType.DMA((4, HPD, MOST_PARTS)),
            pltpu.SemaphoreType.DMA((2, HPD, MOST_PARTS)),
            pltpu.SemaphoreType.DMA((2, HPD, MOST_PARTS)),
            pltpu.SemaphoreType.DMA((2, HPD, MOST_PARTS)),
            pltpu.SemaphoreType.DMA((2, HPD, MOST_PARTS)),
            pltpu.SemaphoreType.DMA((4,)),
            pltpu.SemaphoreType.DMA((4,)),
        ]
    )
    outs = pl.pallas_call(
        kernel,
        out_shape=[jax.ShapeDtypeStruct(shape, bf16)] * 4,
        in_specs=[pl.BlockSpec(memory_space=pl.ANY)] * 6,
        out_specs=[pl.BlockSpec(memory_space=pl.ANY)] * 4,
        scratch_shapes=scratch,
        compiler_params=pltpu.CompilerParams(
            collective_id=0, has_side_effects=True, vmem_limit_bytes=60 * 1024 * 1024
        ),
        cost_estimate=pl.CostEstimate(flops=7_250_000_000, bytes_accessed=12_600_000, transcendentals=4_718_592),
        name="sparse_attention",
    )(*(a.reshape(shape) for a in (query, key_in, value, out_grad)), segment.reshape(NCTX * TPD, TILE), kv_list.T)
    outs = pl.pallas_call(
        hand_over,
        out_shape=[jax.ShapeDtypeStruct(shape, bf16)] * 4,
        in_specs=[pl.BlockSpec(memory_space=pl.ANY)] * 4,
        out_specs=[pl.BlockSpec(memory_space=pl.ANY)] * 4,
        scratch_shapes=[
            pltpu.VMEM((4,) + shape, bf16),
            pltpu.SemaphoreType.DMA((4, 2)),
            pltpu.SemaphoreType.DMA((4, 2)),
        ],
        compiler_params=pltpu.CompilerParams(vmem_limit_bytes=60 * 1024 * 1024),
        name="hand_over",
    )(*outs)
    return tuple(o.reshape(tokens, width) for o in outs)


def solution(mesh):
    tokens = P(("ctx", "head"), None)
    return jax.shard_map(
        body,
        mesh=mesh,
        in_specs=(tokens, tokens, tokens, tokens, P(), P()),
        out_specs=(tokens, tokens, tokens, tokens),
        check_vma=False,
    )
```

```python
import jax
import jax.numpy as jnp
from jax import lax
from jax.experimental import pallas as pl
from jax.experimental.pallas import tpu as pltpu
from jax.sharding import PartitionSpec as P

HEAD_DIM = 128
TILE = 128
LIST = 6
CAP = 2
TPD = 16
NCTX = 16
NHEAD = 8
HPD = 3
NREM = (NCTX - 1) * CAP
SLOTS = TPD + NREM
ROWS = TPD * LIST
HALF = ROWS // 2
MASKED = -1e30
SCALE = HEAD_DIM**-0.5
LOG2E = 1.4426950408889634
MESH = pl.DeviceIdType.MESH

OFFSETS = (
    (0, 1), (2, 3), (0, 3), (2, 1), (1, 0), (3, 2), (3, 0), (1, 2),
    (0, 2), (2, 0), (2, 2), (1, 1), (3, 3), (1, 3), (3, 1),
)

WHOLE = ((0, TILE),)
RISING = ((0, 32), (32, 32), (64, 64))
FALLING = ((0, 64), (64, 32), (96, 32))
PARTS_IN = {(s, h): WHOLE for s in range(2) for h in range(HPD)} | {(0, 0): RISING}
PARTS_BACK = {(s, h): WHOLE for s in range(2) for h in range(HPD)} | {(1, HPD - 1): FALLING}
MOST_PARTS = 3
LATE = {(1, 1, 0): ((1, 2, 0),), (0, 2, 0): ((1, 2, 1), (1, 2, 2))}

T_SLOT, T_TILE = 0, 1
T_LPERM, T_LSAME, T_LLAST = 3, 4, 5
T_RPERM, T_RSAME, T_RLAST = 6, 7, 8
T_BPERM, T_BSAME, T_BLAST = 9, 10, 11
T_EDGE = 12
T_ROWS = 16


def relative(y, z, other):
    return (((other >> 2) - y) & 3) * 4 + (((other & 3) - z) & 3)


def wanted_tiles(me, kv):
    y, z = me // 4, me % 4
    at = lax.broadcasted_iota(jnp.int32, (TILE, 1), 0)
    wide = lax.broadcasted_iota(jnp.int32, (TILE, NCTX * TPD), 1)
    low = jnp.full((1, NCTX * TPD), TPD, jnp.int32)
    high = jnp.full((1, NCTX * TPD), -1, jnp.int32)
    for j in range(LIST):
        row = kv[j : j + 1, :]
        asked = (row >> 4) == me
        low = jnp.where(asked, jnp.minimum(low, row & 15), low)
        high = jnp.where(asked, jnp.maximum(high, row & 15), high)
    step = (at >> 1) + 1
    asker = ((y + (step >> 2)) & 3) * 4 + ((z + (step & 3)) & 3)
    group = (wide >> 4) == asker
    first = jnp.min(jnp.where(group, low, TPD), axis=1, keepdims=True)
    second = jnp.max(jnp.where(group, high, -1), axis=1, keepdims=True)
    return jnp.clip(jnp.where((at & 1) == 0, first, second), 0, TPD - 1)


def diagonal(col):
    eye = lax.broadcasted_iota(jnp.int32, (TILE, TILE), 0) == lax.broadcasted_iota(jnp.int32, (TILE, TILE), 1)
    return jnp.sum(jnp.where(eye, col, 0), axis=0, keepdims=True)


def build_tables(me, kv, seg, want_r, table):
    y, z = me // 4, me % 4
    big = 1 << 20
    sub = lax.broadcasted_iota(jnp.int32, (TILE, TILE), 0)
    lane = lax.broadcasted_iota(jnp.int32, (TILE, TILE), 1)
    at = lax.broadcasted_iota(jnp.int32, (TILE, 1), 0)

    def count(mask):
        return jnp.sum(jnp.where(mask, 1, 0), axis=0, keepdims=True)

    def runs(key_c, key_r, valid_c, valid_r):
        full_c = jnp.where(valid_c, key_c * TILE + at, big)
        full_r = jnp.where(valid_r, key_r * TILE + lane, big)
        place = jnp.sum(jnp.where(full_r < full_c, 1, 0), axis=1, keepdims=True)
        hit = (place == lane) & valid_c
        after = (place + 1 == lane) & valid_c
        perm = jnp.sum(jnp.where(hit, sub, 0), axis=0, keepdims=True)
        key = jnp.sum(jnp.where(hit, key_c + 1, 0), axis=0, keepdims=True)
        before = jnp.sum(jnp.where(after, key_c + 1, 0), axis=0, keepdims=True)
        return perm, jnp.where(key == before, 1, 0)

    wide = lax.broadcasted_iota(jnp.int32, (TILE, NCTX * TPD), 1)
    rows = [kv[j : j + 1, :] for j in range(LIST)]
    want_c = jnp.sum(jnp.where(sub == lane, want_r, 0), axis=1, keepdims=True)
    mine_c = jnp.zeros((TILE, 1), jnp.int32)
    for j in range(LIST):
        here = (wide == me * TPD + (at & 15)) & ((at >> 4) == j)
        mine_c = mine_c + jnp.sum(jnp.where(here, rows[j], 0), axis=1, keepdims=True)
    mine_r = diagonal(mine_c)
    own_c, own_r = mine_c >> 4, mine_r >> 4
    in_c, in_r = mine_c & 15, mine_r & 15
    real_c, real_r = at < ROWS, lane < ROWS
    lowest = jnp.min(jnp.where((own_c == own_r) & real_r, in_r, TPD), axis=1, keepdims=True)
    rank = jnp.where(in_c != lowest, 1, 0)
    slot_c = jnp.where(own_c == me, in_c, TPD + CAP * (relative(y, z, own_c) - 1) + rank)
    slot_r = diagonal(slot_c)
    local_c, local_r = (own_c == me) & real_c, (own_r == me) & real_r
    other_c, other_r = (own_c != me) & real_c, (own_r != me) & real_r
    l_perm, l_same = runs(slot_c, slot_r, local_c, local_r)
    r_perm, r_same = runs(slot_c, slot_r, other_c, other_r)
    asked_c, asked_r = at < NREM, lane < NREM
    b_perm, b_same = runs(want_c, want_r, asked_c, asked_r)
    upto = count((want_c <= lane) & asked_c)
    b_last = jnp.where(count((want_c == lane) & asked_c) > 0, upto, 0)
    edges = []
    for value in (1, 2):
        per_lane = jnp.sum(jnp.where(seg[...] < value, 1, 0), axis=0, keepdims=True)
        edges.append(jnp.sum(per_lane, axis=1, keepdims=True))
    lane_r = lax.broadcasted_iota(jnp.int32, (1, TILE), 1)
    found = {
        T_SLOT: slot_r,
        T_TILE: mine_r,
        T_LPERM: l_perm,
        T_LSAME: l_same,
        T_LLAST: jnp.clip(count((slot_c <= lane) & local_c) - 1, 0, HALF - 1),
        T_RPERM: r_perm,
        T_RSAME: r_same,
        T_RLAST: jnp.clip(count((slot_c - TPD <= lane) & other_c) - 1, 0, HALF - 1),
        T_BPERM: b_perm,
        T_BSAME: b_same,
        T_BLAST: b_last,
        T_EDGE: jnp.where(lane_r == 0, edges[0], edges[1]),
    }
    none = jnp.zeros((1, TILE), jnp.int32)
    table[...] = jnp.concatenate([found.get(r, none) for r in range(T_ROWS)], axis=0)


def dot_nt(a, b):
    return lax.dot_general(a, b, (((1,), (1,)), ((), ())), preferred_element_type=jnp.float32)


def dot_nn(a, b):
    return lax.dot_general(a, b, (((1,), (0,)), ((), ())), preferred_element_type=jnp.float32)


def dot_tn(a, b):
    return lax.dot_general(a, b, (((0,), (0,)), ((), ())), preferred_element_type=jnp.float32)


def attend(tab, me, q, g, k_all, v_all, o_out, dq_out, c_key, c_value):
    edge1, edge2 = tab[T_EDGE, 0], tab[T_EDGE, 1]
    end = NCTX * TPD * TILE

    def one(i, carry):
        query, grad = q[i], g[i]
        slots = [tab[T_SLOT, j * TPD + i] for j in range(LIST)]
        keys = jnp.concatenate([k_all[s] for s in slots], axis=0)
        values = jnp.concatenate([v_all[s] for s in slots], axis=0)
        scores = dot_nt(query, keys) * (SCALE * LOG2E)
        at = (me * TPD + i) * TILE + lax.broadcasted_iota(jnp.int32, (TILE, TILE), 0)
        start = jnp.where(at >= edge2, edge2, jnp.where(at >= edge1, edge1, 0))
        stop = jnp.where(at >= edge2, end, jnp.where(at >= edge1, edge2, edge1))
        lane = lax.broadcasted_iota(jnp.int32, (TILE, TILE), 1)
        parts = []
        for j in range(LIST):
            key_at = tab[T_TILE, j * TPD + i] * TILE + lane
            allowed = (key_at >= start) & (key_at < stop)
            parts.append(jnp.where(allowed, scores[:, j * TILE : (j + 1) * TILE], MASKED))
        scores = jnp.concatenate(parts, axis=1)
        top = jnp.max(scores, axis=1, keepdims=True)
        expd = jnp.exp2(scores - top)
        probs = expd * (1.0 / jnp.sum(expd, axis=1, keepdims=True))
        low = probs.astype(jnp.bfloat16)
        attended = dot_nn(low, values).astype(jnp.bfloat16)
        o_out[i] = attended
        grad_probs = dot_nt(grad, values)
        row_dot = jnp.sum(grad.astype(jnp.float32) * attended.astype(jnp.float32), axis=1, keepdims=True)
        grad_scores = (probs * (grad_probs - row_dot)).astype(jnp.bfloat16)
        dq_out[i] = (dot_nn(grad_scores, keys) * SCALE).astype(jnp.bfloat16)
        key_part = (dot_tn(grad_scores, query) * SCALE).astype(jnp.bfloat16)
        value_part = dot_tn(low, grad).astype(jnp.bfloat16)
        for j in range(LIST):
            c_key[j * TPD + i] = key_part[j * TILE : (j + 1) * TILE]
            c_value[j * TPD + i] = value_part[j * TILE : (j + 1) * TILE]
        return carry

    lax.fori_loop(0, TPD, one, 0)


def run_sums(tab, perm, same, count, parts, out, shift=0, rows=TILE):
    def one(p, total):
        total = jnp.where(tab[same, p] == 1, total, 0.0) + parts[tab[perm, p]].astype(jnp.float32)
        out[p + shift, pl.ds(0, rows)] = total.astype(out.dtype)
        return total

    lax.fori_loop(0, count, one, jnp.zeros((rows, HEAD_DIM), jnp.float32))


def wait_bytes(ref, sem):
    pltpu.make_async_copy(ref, ref, sem).wait()


def kernel(q_in, k_in, v_in, g_in, seg_in, kv_in, o_out, dq_out, dk_out, dv_out, *scratch):
    it = iter(scratch)

    def take(n):
        return [next(it) for _ in range(n)]

    def take_parts(parts):
        return {(s, h): take(len(parts[s, h])) for s in range(2) for h in range(HPD)}

    q_loc, g_loc = take(HPD), take(HPD)
    kv_loc, kv_back = take_parts(PARTS_IN), take_parts(PARTS_BACK)
    k_all, v_all = take(HPD), take(HPD)
    k_stage, v_stage = take(HPD), take(HPD)
    o_stage, dq_stage, dk_stage, dv_stage = take(HPD), take(HPD), take(HPD), take(HPD)
    k_sum, v_sum = take(HPD), take(HPD)
    c_key, c_value, run_local, run_remote, run_back = take(5)
    kv, seg, table, want_table, tab, want_tab, t_sem = take(7)
    x_send, x_recv, c_send, c_recv, b_send, b_recv, y_send, y_recv = take(8)

    me, head = lax.axis_index("ctx"), lax.axis_index("head")
    y, z = me // 4, me % 4

    fetches = [pltpu.make_async_copy(kv_in, kv, t_sem.at[0]), pltpu.make_async_copy(seg_in, seg, t_sem.at[1])]
    for fetch in fetches:
        fetch.start()

    barrier = pltpu.get_barrier_semaphore()
    for d in range(1, NHEAD):
        pl.semaphore_signal(barrier, inc=1, device_id=(me, (head + d) % NHEAD), device_id_type=MESH)
    for dy, dz in OFFSETS:
        peer = ((y + dy) % 4) * 4 + (z + dz) % 4
        pl.semaphore_signal(barrier, inc=1, device_id=(peer, head), device_id_type=MESH)
    pl.semaphore_wait(barrier, NHEAD - 1 + NCTX - 1)

    def columns(owner, h):
        return pl.ds(pl.multiple_of((owner * HPD + h) * HEAD_DIM, HEAD_DIM), HEAD_DIM)

    def pair(index):
        return pl.ds(2 * index, 2)

    def send_in(src, dst, rows, h, send_sem, recv_sem):
        for d in range(1, NHEAD):
            peer = (head + d) % NHEAD
            pltpu.make_async_remote_copy(
                src_ref=src.at[:, pl.ds(*rows), columns(peer, h)],
                dst_ref=dst.at[pair(head)],
                send_sem=send_sem,
                recv_sem=recv_sem,
                device_id=(me, peer),
                device_id_type=MESH,
            ).start()
        pltpu.make_async_copy(src.at[:, pl.ds(*rows), columns(head, h)], dst.at[pair(head)], recv_sem).start()

    def send_kv(s, h, n=0):
        rows = PARTS_IN[s, h][n]
        send_in((k_in, v_in)[s], kv_loc[s, h][n], rows, h, x_send.at[2 + s], x_recv.at[2 + s, h, n])

    def send_qg(h):
        send_in(q_in, q_loc[h], WHOLE[0], h, x_send.at[0], x_recv.at[0, h, 0])
        send_in(g_in, g_loc[h], WHOLE[0], h, x_send.at[1], x_recv.at[1, h, 0])

    def send_out(a, h, rows):
        src, dst = (o_stage, dq_stage, dk_stage, dv_stage)[a][h], (o_out, dq_out, dk_out, dv_out)[a]
        for d in range(1, NHEAD):
            peer = (head + d) % NHEAD
            pltpu.make_async_remote_copy(
                src_ref=src.at[pair(peer), pl.ds(*rows)],
                dst_ref=dst.at[:, pl.ds(*rows), columns(head, h)],
                send_sem=y_send.at[a],
                recv_sem=y_recv.at[a],
                device_id=(me, peer),
                device_id_type=MESH,
            ).start()
        pltpu.make_async_copy(
            src.at[pair(head), pl.ds(*rows)], dst.at[:, pl.ds(*rows), columns(head, h)], y_recv.at[a]
        ).start()

    def send_ctx(stage, landing, base, rows, landing_rows, send_sem, recv_sem):
        for dy, dz in OFFSETS:
            there = dy * 4 + dz - 1
            here = ((-dy) % 4) * 4 + (-dz) % 4 - 1
            peer = ((y + dy) % 4) * 4 + (z + dz) % 4
            pltpu.make_async_remote_copy(
                src_ref=stage.at[pl.ds(CAP * there, CAP), pl.ds(*rows)],
                dst_ref=landing.at[pl.ds(base + CAP * here, CAP), pl.ds(*landing_rows)],
                send_sem=send_sem,
                recv_sem=recv_sem,
                device_id=(peer, head),
                device_id_type=MESH,
            ).start()

    def wait_kv(s, h, n=0):
        wait_bytes(kv_loc[s, h][n], x_recv.at[2 + s, h, n])

    def forward_tiles(s, h, n=0):
        stage, everything = (k_stage, v_stage)[s][h], (k_all, v_all)[s][h]
        rows, local = PARTS_IN[s, h][n], kv_loc[s, h][n]

        def pack(p, carry):
            stage[p, pl.ds(*rows)] = local[want_tab[0, p]]
            return carry

        lax.fori_loop(0, NREM, pack, 0)
        send_ctx(stage, everything, TPD, rows, rows, c_send.at[s, h, n], c_recv.at[s, h, n])

        def keep(p, carry):
            everything[p, pl.ds(*rows)] = local[p]
            return carry

        lax.fori_loop(0, TPD, keep, 0)

    def forward(s, h, n=0):
        wait_kv(s, h, n)
        forward_tiles(s, h, n)

    send_kv(0, 0, 0)
    fetches[0].wait()
    want = diagonal(wanted_tiles(me, kv))
    want_table[...] = jnp.broadcast_to(want, (8, TILE))
    to_scalar = pltpu.make_async_copy(want_table, want_tab, t_sem.at[2])
    to_scalar.start()
    send_kv(0, 0, 1)
    send_kv(0, 0, 2)
    to_scalar.wait()
    send_kv(1, 0)
    forward(0, 0, 0)
    send_kv(0, 1)
    forward(0, 0, 1)
    send_kv(1, 1)
    forward(0, 0, 2)
    send_kv(0, 2)
    forward(1, 0)
    send_kv(1, 2)
    fetches[1].wait()
    build_tables(me, kv, seg, want, table)
    to_scalar = pltpu.make_async_copy(table, tab, t_sem.at[3])
    to_scalar.start()
    forward(0, 1)
    send_qg(0)
    forward(1, 1)
    send_qg(1)
    forward(0, 2)
    send_qg(2)
    forward(1, 2)
    to_scalar.wait()

    def send_back(s, h, n):
        rows, stage, landing = PARTS_BACK[s, h][n], (k_stage, v_stage)[s][h], kv_back[s, h][n]
        send_ctx(stage, landing, 0, rows, (0, rows[1]), b_send.at[s, h, n], b_recv.at[s, h, n])

    for h in range(HPD):
        wait_bytes(q_loc[h], x_recv.at[0, h, 0])
        wait_bytes(g_loc[h], x_recv.at[1, h, 0])
        for s in range(2):
            for n, rows in enumerate(PARTS_IN[s, h]):
                wait_bytes((k_all, v_all)[s][h].at[pl.ds(TPD, NREM), pl.ds(*rows)], c_recv.at[s, h, n])
        attend(tab, me, q_loc[h], g_loc[h], k_all[h], v_all[h], o_stage[h], dq_stage[h], c_key, c_value)
        send_out(0, h, WHOLE[0])
        send_out(1, h, WHOLE[0])
        for s in range(2):
            stage = (k_stage, v_stage)[s][h]
            run_sums(tab, T_RPERM, T_RSAME, HALF, (c_key, c_value)[s], run_remote)
            for n, rows in enumerate(PARTS_IN[s, h]):
                wait_bytes(stage.at[:, pl.ds(*rows)], c_send.at[s, h, n])

            def fill(p, carry, stage=stage):
                stage[p] = run_remote[tab[T_RLAST, p]]
                return carry

            lax.fori_loop(0, NREM, fill, 0)
            for n in range(len(PARTS_BACK[s, h])):
                if (s, h, n) not in sum(LATE.values(), ()):
                    send_back(s, h, n)
        for s in range(2):
            sums = (k_sum, v_sum)[s][h]
            run_sums(tab, T_LPERM, T_LSAME, HALF, (c_key, c_value)[s], run_local)

            def settle(p, carry, sums=sums):
                sums[p] = run_local[tab[T_LLAST, p]]
                return carry

            lax.fori_loop(0, TPD, settle, 0)

    run_back[0] = jnp.zeros((TILE, HEAD_DIM), jnp.float32)
    for h in range(HPD):
        for s in range(2):
            sums, stage = (k_sum, v_sum)[s][h], (dk_stage, dv_stage)[s][h]
            for n, rows in enumerate(PARTS_BACK[s, h]):
                back = kv_back[s, h][n]
                wait_bytes(back, b_recv.at[s, h, n])
                for later in LATE.get((s, h, n), ()):
                    send_back(*later)
                run_sums(tab, T_BPERM, T_BSAME, NREM, back, run_back, shift=1, rows=rows[1])

                def finish(p, carry, sums=sums, stage=stage, rows=rows):
                    total = sums[p, pl.ds(*rows)] + run_back[tab[T_BLAST, p], pl.ds(0, rows[1])]
                    stage[p, pl.ds(*rows)] = total.astype(jnp.bfloat16)
                    return carry

                lax.fori_loop(0, TPD, finish, 0)
                send_out(2 + s, h, rows)

    sent = CAP * (NHEAD - 1) * HPD
    for a in range(4):
        wait_bytes(k_all[0].at[pl.ds(0, sent)], x_send.at[a])
        wait_bytes(k_all[0].at[pl.ds(0, sent)], y_send.at[a])
        wait_bytes((o_out, dq_out, dk_out, dv_out)[a], y_recv.at[a])
    for s in range(2):
        for h in range(HPD):
            for n, rows in enumerate(PARTS_BACK[s, h]):
                wait_bytes((k_stage, v_stage)[s][h].at[:, pl.ds(*rows)], b_send.at[s, h, n])


def hand_over(*refs):
    copies = [
        pltpu.make_async_copy(refs[a].at[p], refs[4 + a].at[p], refs[8].at[a, p]) for a in range(4) for p in range(2)
    ]
    for copy in copies:
        copy.start()
    for copy in copies:
        copy.wait()


def body(query, key_in, value, out_grad, segment, kv_list):
    tokens, width = query.shape
    shape = (tokens // TILE, TILE, width)
    bf16, f32 = jnp.bfloat16, jnp.float32

    def vmem(n, dtype=bf16, rows=TILE):
        return pltpu.VMEM((n, rows, HEAD_DIM), dtype)

    def vmem_parts(n, parts):
        return [vmem(n, rows=rows) for s in range(2) for h in range(HPD) for _, rows in parts[s, h]]

    scratch = (
        [vmem(TPD)] * (2 * HPD)
        + vmem_parts(TPD, PARTS_IN)
        + vmem_parts(NREM, PARTS_BACK)
        + [vmem(SLOTS)] * (2 * HPD)
        + [vmem(NREM)] * (2 * HPD)
        + [vmem(TPD)] * (4 * HPD)
        + [vmem(TPD, f32)] * (2 * HPD)
        + [vmem(ROWS), vmem(ROWS), vmem(HALF, f32), vmem(HALF), vmem(NREM + 1, f32)]
        + [
            pltpu.VMEM((LIST, NCTX * TPD), jnp.int32),
            pltpu.VMEM((NCTX * TPD, TILE), jnp.int32),
            pltpu.VMEM((T_ROWS, TILE), jnp.int32),
            pltpu.VMEM((8, TILE), jnp.int32),
            pltpu.SMEM((T_ROWS, TILE), jnp.int32),
            pltpu.SMEM((8, TILE), jnp.int32),
            pltpu.SemaphoreType.DMA((4,)),
            pltpu.SemaphoreType.DMA((4,)),
            pltpu.SemaphoreType.DMA((4, HPD, MOST_PARTS)),
            pltpu.SemaphoreType.DMA((2, HPD, MOST_PARTS)),
            pltpu.SemaphoreType.DMA((2, HPD, MOST_PARTS)),
            pltpu.SemaphoreType.DMA((2, HPD, MOST_PARTS)),
            pltpu.SemaphoreType.DMA((2, HPD, MOST_PARTS)),
            pltpu.SemaphoreType.DMA((4,)),
            pltpu.SemaphoreType.DMA((4,)),
        ]
    )
    outs = pl.pallas_call(
        kernel,
        out_shape=[pltpu.VMEM(shape, bf16)] * 4,
        in_specs=[pl.BlockSpec(memory_space=pl.ANY)] * 6,
        out_specs=[pl.BlockSpec(memory_space=pl.ANY)] * 4,
        scratch_shapes=scratch,
        compiler_params=pltpu.CompilerParams(
            collective_id=0, has_side_effects=True, vmem_limit_bytes=52 * 1024 * 1024
        ),
        cost_estimate=pl.CostEstimate(flops=7_250_000_000, bytes_accessed=12_600_000, transcendentals=4_718_592),
        name="sparse_attention",
    )(*(a.reshape(shape) for a in (query, key_in, value, out_grad)), segment.reshape(NCTX * TPD, TILE), kv_list.T)
    outs = pl.pallas_call(
        hand_over,
        out_shape=[jax.ShapeDtypeStruct(shape, bf16)] * 4,
        in_specs=[pl.BlockSpec(memory_space=pl.ANY)] * 4,
        out_specs=[pl.BlockSpec(memory_space=pl.ANY)] * 4,
        scratch_shapes=[pltpu.SemaphoreType.DMA((4, 2))],
        compiler_params=pltpu.CompilerParams(vmem_limit_bytes=4 * 1024 * 1024),
        name="hand_over",
    )(*outs)
    return tuple(o.reshape(tokens, width) for o in outs)


def solution(mesh):
    tokens = P(("ctx", "head"), None)
    return jax.shard_map(
        body,
        mesh=mesh,
        in_specs=(tokens, tokens, tokens, tokens, P(), P()),
        out_specs=(tokens, tokens, tokens, tokens),
        check_vma=False,
    )
```

```python
import jax
import jax.numpy as jnp
from jax import lax
from jax.experimental import pallas as pl
from jax.experimental.pallas import tpu as pltpu
from jax.sharding import PartitionSpec as P

HEAD_DIM = 128
TILE = 128
LIST = 6
CAP = 2
TPD = 16
NCTX = 16
NHEAD = 8
HPD = 3
NREM = (NCTX - 1) * CAP
SLOTS = TPD + NREM
ROWS = TPD * LIST
HALF = ROWS // 2
MASKED = -1e30
SCALE = HEAD_DIM**-0.5
LOG2E = 1.4426950408889634
MESH = pl.DeviceIdType.MESH

OFFSETS = (
    (1, 1), (3, 3), (1, 3), (3, 1), (0, 2), (2, 0), (2, 2), (1, 2), (3, 0), (3, 2), (1, 0), (2, 1), (0, 3), (2, 3), (0, 1),
)

AROUND = ((2, 0), (1, 0), (3, 0), (2, 1), (3, 1), (1, 1), (0, 1))

WHOLE = ((0, TILE),)
RISING = ((0, 32), (32, 32), (64, 64))
FALLING = ((0, 64), (64, 32), (96, 32))
PARTS_IN = {(s, h): WHOLE for s in range(2) for h in range(HPD)} | {(0, 0): RISING}
PARTS_BACK = {(s, h): WHOLE for s in range(2) for h in range(HPD)} | {(1, HPD - 1): FALLING}
MOST_PARTS = 3
LATE = {(1, 1, 0): ((1, 2, 0),), (0, 2, 0): ((1, 2, 1), (1, 2, 2))}

T_SLOT, T_TILE = 0, 1
T_LPERM, T_LSAME, T_LLAST = 3, 4, 5
T_RPERM, T_RSAME, T_RLAST = 6, 7, 8
T_BPERM, T_BSAME, T_BLAST = 9, 10, 11
T_EDGE = 12
T_ROWS = 16


def relative(y, z, other):
    return (((other >> 2) - y) & 3) * 4 + (((other & 3) - z) & 3)


def wanted_tiles(me, kv):
    y, z = me // 4, me % 4
    at = lax.broadcasted_iota(jnp.int32, (TILE, 1), 0)
    wide = lax.broadcasted_iota(jnp.int32, (TILE, NCTX * TPD), 1)
    low = jnp.full((1, NCTX * TPD), TPD, jnp.int32)
    high = jnp.full((1, NCTX * TPD), -1, jnp.int32)
    for j in range(LIST):
        row = kv[j : j + 1, :]
        asked = (row >> 4) == me
        low = jnp.where(asked, jnp.minimum(low, row & 15), low)
        high = jnp.where(asked, jnp.maximum(high, row & 15), high)
    step = (at >> 1) + 1
    asker = ((y + (step >> 2)) & 3) * 4 + ((z + (step & 3)) & 3)
    group = (wide >> 4) == asker
    first = jnp.min(jnp.where(group, low, TPD), axis=1, keepdims=True)
    second = jnp.max(jnp.where(group, high, -1), axis=1, keepdims=True)
    return jnp.clip(jnp.where((at & 1) == 0, first, second), 0, TPD - 1)


def diagonal(col):
    eye = lax.broadcasted_iota(jnp.int32, (TILE, TILE), 0) == lax.broadcasted_iota(jnp.int32, (TILE, TILE), 1)
    return jnp.sum(jnp.where(eye, col, 0), axis=0, keepdims=True)


def build_tables(me, kv, seg, want_r, table):
    y, z = me // 4, me % 4
    big = 1 << 20
    sub = lax.broadcasted_iota(jnp.int32, (TILE, TILE), 0)
    lane = lax.broadcasted_iota(jnp.int32, (TILE, TILE), 1)
    at = lax.broadcasted_iota(jnp.int32, (TILE, 1), 0)

    def count(mask):
        return jnp.sum(jnp.where(mask, 1, 0), axis=0, keepdims=True)

    def runs(key_c, key_r, valid_c, valid_r):
        full_c = jnp.where(valid_c, key_c * TILE + at, big)
        full_r = jnp.where(valid_r, key_r * TILE + lane, big)
        place = jnp.sum(jnp.where(full_r < full_c, 1, 0), axis=1, keepdims=True)
        hit = (place == lane) & valid_c
        after = (place + 1 == lane) & valid_c
        perm = jnp.sum(jnp.where(hit, sub, 0), axis=0, keepdims=True)
        key = jnp.sum(jnp.where(hit, key_c + 1, 0), axis=0, keepdims=True)
        before = jnp.sum(jnp.where(after, key_c + 1, 0), axis=0, keepdims=True)
        return perm, jnp.where(key == before, 1, 0)

    wide = lax.broadcasted_iota(jnp.int32, (TILE, NCTX * TPD), 1)
    rows = [kv[j : j + 1, :] for j in range(LIST)]
    want_c = jnp.sum(jnp.where(sub == lane, want_r, 0), axis=1, keepdims=True)
    mine_c = jnp.zeros((TILE, 1), jnp.int32)
    for j in range(LIST):
        here = (wide == me * TPD + (at & 15)) & ((at >> 4) == j)
        mine_c = mine_c + jnp.sum(jnp.where(here, rows[j], 0), axis=1, keepdims=True)
    mine_r = diagonal(mine_c)
    own_c, own_r = mine_c >> 4, mine_r >> 4
    in_c, in_r = mine_c & 15, mine_r & 15
    real_c, real_r = at < ROWS, lane < ROWS
    lowest = jnp.min(jnp.where((own_c == own_r) & real_r, in_r, TPD), axis=1, keepdims=True)
    rank = jnp.where(in_c != lowest, 1, 0)
    slot_c = jnp.where(own_c == me, in_c, TPD + CAP * (relative(y, z, own_c) - 1) + rank)
    slot_r = diagonal(slot_c)
    local_c, local_r = (own_c == me) & real_c, (own_r == me) & real_r
    other_c, other_r = (own_c != me) & real_c, (own_r != me) & real_r
    l_perm, l_same = runs(slot_c, slot_r, local_c, local_r)
    r_perm, r_same = runs(slot_c, slot_r, other_c, other_r)
    asked_c, asked_r = at < NREM, lane < NREM
    b_perm, b_same = runs(want_c, want_r, asked_c, asked_r)
    upto = count((want_c <= lane) & asked_c)
    b_last = jnp.where(count((want_c == lane) & asked_c) > 0, upto, 0)
    edges = []
    for value in (1, 2):
        per_lane = jnp.sum(jnp.where(seg[...] < value, 1, 0), axis=0, keepdims=True)
        edges.append(jnp.sum(per_lane, axis=1, keepdims=True))
    lane_r = lax.broadcasted_iota(jnp.int32, (1, TILE), 1)
    found = {
        T_SLOT: slot_r,
        T_TILE: mine_r,
        T_LPERM: l_perm,
        T_LSAME: l_same,
        T_LLAST: jnp.clip(count((slot_c <= lane) & local_c) - 1, 0, HALF - 1),
        T_RPERM: r_perm,
        T_RSAME: r_same,
        T_RLAST: jnp.clip(count((slot_c - TPD <= lane) & other_c) - 1, 0, HALF - 1),
        T_BPERM: b_perm,
        T_BSAME: b_same,
        T_BLAST: b_last,
        T_EDGE: jnp.where(lane_r == 0, edges[0], edges[1]),
    }
    none = jnp.zeros((1, TILE), jnp.int32)
    table[...] = jnp.concatenate([found.get(r, none) for r in range(T_ROWS)], axis=0)


def dot_nt(a, b):
    return lax.dot_general(a, b, (((1,), (1,)), ((), ())), preferred_element_type=jnp.float32)


def dot_nn(a, b):
    return lax.dot_general(a, b, (((1,), (0,)), ((), ())), preferred_element_type=jnp.float32)


def dot_tn(a, b):
    return lax.dot_general(a, b, (((0,), (0,)), ((), ())), preferred_element_type=jnp.float32)


def attend(tab, me, q, g, k_all, v_all, o_out, dq_out, c_key, c_value):
    edge1, edge2 = tab[T_EDGE, 0], tab[T_EDGE, 1]
    end = NCTX * TPD * TILE

    def one(i, carry):
        query, grad = q[i], g[i]
        slots = [tab[T_SLOT, j * TPD + i] for j in range(LIST)]
        keys = jnp.concatenate([k_all[s] for s in slots], axis=0)
        values = jnp.concatenate([v_all[s] for s in slots], axis=0)
        scores = dot_nt(query, keys) * (SCALE * LOG2E)
        at = (me * TPD + i) * TILE + lax.broadcasted_iota(jnp.int32, (TILE, TILE), 0)
        start = jnp.where(at >= edge2, edge2, jnp.where(at >= edge1, edge1, 0))
        stop = jnp.where(at >= edge2, end, jnp.where(at >= edge1, edge2, edge1))
        lane = lax.broadcasted_iota(jnp.int32, (TILE, TILE), 1)
        parts = []
        for j in range(LIST):
            key_at = tab[T_TILE, j * TPD + i] * TILE + lane
            allowed = (key_at >= start) & (key_at < stop)
            parts.append(jnp.where(allowed, scores[:, j * TILE : (j + 1) * TILE], MASKED))
        scores = jnp.concatenate(parts, axis=1)
        top = jnp.max(scores, axis=1, keepdims=True)
        expd = jnp.exp2(scores - top)
        probs = expd * (1.0 / jnp.sum(expd, axis=1, keepdims=True))
        low = probs.astype(jnp.bfloat16)
        attended = dot_nn(low, values).astype(jnp.bfloat16)
        o_out[i] = attended
        grad_probs = dot_nt(grad, values)
        row_dot = jnp.sum(grad.astype(jnp.float32) * attended.astype(jnp.float32), axis=1, keepdims=True)
        grad_scores = (probs * (grad_probs - row_dot)).astype(jnp.bfloat16)
        dq_out[i] = (dot_nn(grad_scores, keys) * SCALE).astype(jnp.bfloat16)
        key_part = (dot_tn(grad_scores, query) * SCALE).astype(jnp.bfloat16)
        value_part = dot_tn(low, grad).astype(jnp.bfloat16)
        for j in range(LIST):
            c_key[j * TPD + i] = key_part[j * TILE : (j + 1) * TILE]
            c_value[j * TPD + i] = value_part[j * TILE : (j + 1) * TILE]
        return carry

    lax.fori_loop(0, TPD, one, 0)


def run_sums(tab, perm, same, count, parts, out, shift=0, rows=TILE):
    def one(p, total):
        total = jnp.where(tab[same, p] == 1, total, 0.0) + parts[tab[perm, p]].astype(jnp.float32)
        out[p + shift, pl.ds(0, rows)] = total.astype(out.dtype)
        return total

    lax.fori_loop(0, count, one, jnp.zeros((rows, HEAD_DIM), jnp.float32))


def wait_bytes(ref, sem):
    pltpu.make_async_copy(ref, ref, sem).wait()


def kernel(q_in, k_in, v_in, g_in, seg_in, kv_in, o_out, dq_out, dk_out, dv_out, *scratch):
    it = iter(scratch)

    def take(n):
        return [next(it) for _ in range(n)]

    def take_parts(parts):
        return {(s, h): take(len(parts[s, h])) for s in range(2) for h in range(HPD)}

    q_loc, g_loc = take(HPD), take(HPD)
    kv_loc, kv_back = take_parts(PARTS_IN), take_parts(PARTS_BACK)
    k_all, v_all = take(HPD), take(HPD)
    k_stage, v_stage = take(HPD), take(HPD)
    o_stage, dq_stage, dk_stage, dv_stage = take(HPD), take(HPD), take(HPD), take(HPD)
    k_sum, v_sum = take(HPD), take(HPD)
    c_key, c_value, run_local, run_remote, run_back = take(5)
    kv, seg, table, want_table, tab, want_tab, t_sem = take(7)
    x_send, x_recv, c_send, c_recv, b_send, b_recv, y_send, y_recv = take(8)

    me, head = lax.axis_index("ctx"), lax.axis_index("head")
    y, z, core = me // 4, me % 4, head % 2

    fetches = [pltpu.make_async_copy(kv_in, kv, t_sem.at[0]), pltpu.make_async_copy(seg_in, seg, t_sem.at[1])]
    for fetch in fetches:
        fetch.start()

    barrier = pltpu.get_barrier_semaphore()
    for d in range(1, NHEAD):
        pl.semaphore_signal(barrier, inc=1, device_id=(me, (head + d) % NHEAD), device_id_type=MESH)
    for dy, dz in OFFSETS:
        peer = ((y + dy) % 4) * 4 + (z + dz) % 4
        pl.semaphore_signal(barrier, inc=1, device_id=(peer, head), device_id_type=MESH)
    pl.semaphore_wait(barrier, NHEAD - 1 + NCTX - 1)

    def neighbour(chips, cores):
        along = jnp.where(core == 0, chips, (4 - chips) % 4)
        return ((head // 2 + along) % 4) * 2 + (core + cores) % 2

    def columns(owner, h):
        return pl.ds(pl.multiple_of((owner * HPD + h) * HEAD_DIM, HEAD_DIM), HEAD_DIM)

    def pair(index):
        return pl.ds(2 * index, 2)

    def send_in(src, dst, rows, h, send_sem, recv_sem):
        for chips, cores in AROUND:
            peer = neighbour(chips, cores)
            pltpu.make_async_remote_copy(
                src_ref=src.at[:, pl.ds(*rows), columns(peer, h)],
                dst_ref=dst.at[pair(head)],
                send_sem=send_sem,
                recv_sem=recv_sem,
                device_id=(me, peer),
                device_id_type=MESH,
            ).start()
        pltpu.make_async_copy(src.at[:, pl.ds(*rows), columns(head, h)], dst.at[pair(head)], recv_sem).start()

    def send_kv(s, h, n=0):
        rows = PARTS_IN[s, h][n]
        send_in((k_in, v_in)[s], kv_loc[s, h][n], rows, h, x_send.at[2 + s], x_recv.at[2 + s, h, n])

    def send_qg(h):
        send_in(q_in, q_loc[h], WHOLE[0], h, x_send.at[0], x_recv.at[0, h, 0])
        send_in(g_in, g_loc[h], WHOLE[0], h, x_send.at[1], x_recv.at[1, h, 0])

    def send_out(a, h, rows):
        src, dst = (o_stage, dq_stage, dk_stage, dv_stage)[a][h], (o_out, dq_out, dk_out, dv_out)[a]
        for chips, cores in AROUND:
            peer = neighbour(chips, cores)
            pltpu.make_async_remote_copy(
                src_ref=src.at[pair(peer), pl.ds(*rows)],
                dst_ref=dst.at[:, pl.ds(*rows), columns(head, h)],
                send_sem=y_send.at[a],
                recv_sem=y_recv.at[a],
                device_id=(me, peer),
                device_id_type=MESH,
            ).start()
        pltpu.make_async_copy(
            src.at[pair(head), pl.ds(*rows)], dst.at[:, pl.ds(*rows), columns(head, h)], y_recv.at[a]
        ).start()

    def send_ctx(stage, landing, base, rows, landing_rows, send_sem, recv_sem):
        for one, two in OFFSETS:
            dy, dz = jnp.where(core == 0, one, two), jnp.where(core == 0, two, one)
            there = dy * 4 + dz - 1
            here = ((4 - dy) % 4) * 4 + (4 - dz) % 4 - 1
            peer = ((y + dy) % 4) * 4 + (z + dz) % 4
            pltpu.make_async_remote_copy(
                src_ref=stage.at[pl.ds(CAP * there, CAP), pl.ds(*rows)],
                dst_ref=landing.at[pl.ds(base + CAP * here, CAP), pl.ds(*landing_rows)],
                send_sem=send_sem,
                recv_sem=recv_sem,
                device_id=(peer, head),
                device_id_type=MESH,
            ).start()

    def wait_kv(s, h, n=0):
        wait_bytes(kv_loc[s, h][n], x_recv.at[2 + s, h, n])

    def forward_tiles(s, h, n=0):
        stage, everything = (k_stage, v_stage)[s][h], (k_all, v_all)[s][h]
        rows, local = PARTS_IN[s, h][n], kv_loc[s, h][n]

        def pack(p, carry):
            stage[p, pl.ds(*rows)] = local[want_tab[0, p]]
            return carry

        lax.fori_loop(0, NREM, pack, 0)
        send_ctx(stage, everything, TPD, rows, rows, c_send.at[s, h, n], c_recv.at[s, h, n])

        def keep(p, carry):
            everything[p, pl.ds(*rows)] = local[p]
            return carry

        lax.fori_loop(0, TPD, keep, 0)

    def forward(s, h, n=0):
        wait_kv(s, h, n)
        forward_tiles(s, h, n)

    send_kv(0, 0, 0)
    fetches[0].wait()
    want = diagonal(wanted_tiles(me, kv))
    want_table[...] = jnp.broadcast_to(want, (8, TILE))
    to_scalar = pltpu.make_async_copy(want_table, want_tab, t_sem.at[2])
    to_scalar.start()
    send_kv(0, 0, 1)
    send_kv(0, 0, 2)
    to_scalar.wait()
    send_kv(1, 0)
    forward(0, 0, 0)
    send_kv(0, 1)
    forward(0, 0, 1)
    send_kv(1, 1)
    forward(0, 0, 2)
    send_kv(0, 2)
    forward(1, 0)
    send_kv(1, 2)
    fetches[1].wait()
    build_tables(me, kv, seg, want, table)
    to_scalar = pltpu.make_async_copy(table, tab, t_sem.at[3])
    to_scalar.start()
    forward(0, 1)
    send_qg(0)
    forward(1, 1)
    send_qg(1)
    forward(0, 2)
    send_qg(2)
    forward(1, 2)
    to_scalar.wait()

    def send_back(s, h, n):
        rows, stage, landing = PARTS_BACK[s, h][n], (k_stage, v_stage)[s][h], kv_back[s, h][n]
        send_ctx(stage, landing, 0, rows, (0, rows[1]), b_send.at[s, h, n], b_recv.at[s, h, n])

    for h in range(HPD):
        wait_bytes(q_loc[h], x_recv.at[0, h, 0])
        wait_bytes(g_loc[h], x_recv.at[1, h, 0])
        for s in range(2):
            for n, rows in enumerate(PARTS_IN[s, h]):
                wait_bytes((k_all, v_all)[s][h].at[pl.ds(TPD, NREM), pl.ds(*rows)], c_recv.at[s, h, n])
        attend(tab, me, q_loc[h], g_loc[h], k_all[h], v_all[h], o_stage[h], dq_stage[h], c_key, c_value)
        send_out(0, h, WHOLE[0])
        send_out(1, h, WHOLE[0])
        for s in range(2):
            stage = (k_stage, v_stage)[s][h]
            run_sums(tab, T_RPERM, T_RSAME, HALF, (c_key, c_value)[s], run_remote)
            for n, rows in enumerate(PARTS_IN[s, h]):
                wait_bytes(stage.at[:, pl.ds(*rows)], c_send.at[s, h, n])

            def fill(p, carry, stage=stage):
                stage[p] = run_remote[tab[T_RLAST, p]]
                return carry

            lax.fori_loop(0, NREM, fill, 0)
            for n in range(len(PARTS_BACK[s, h])):
                if (s, h, n) not in sum(LATE.values(), ()):
                    send_back(s, h, n)
        for s in range(2):
            sums = (k_sum, v_sum)[s][h]
            run_sums(tab, T_LPERM, T_LSAME, HALF, (c_key, c_value)[s], run_local)

            def settle(p, carry, sums=sums):
                sums[p] = run_local[tab[T_LLAST, p]]
                return carry

            lax.fori_loop(0, TPD, settle, 0)

    run_back[0] = jnp.zeros((TILE, HEAD_DIM), jnp.float32)
    for h in range(HPD):
        for s in range(2):
            sums, stage = (k_sum, v_sum)[s][h], (dk_stage, dv_stage)[s][h]
            for n, rows in enumerate(PARTS_BACK[s, h]):
                back = kv_back[s, h][n]
                wait_bytes(back, b_recv.at[s, h, n])
                for later in LATE.get((s, h, n), ()):
                    send_back(*later)
                run_sums(tab, T_BPERM, T_BSAME, NREM, back, run_back, shift=1, rows=rows[1])

                def finish(p, carry, sums=sums, stage=stage, rows=rows):
                    total = sums[p, pl.ds(*rows)] + run_back[tab[T_BLAST, p], pl.ds(0, rows[1])]
                    stage[p, pl.ds(*rows)] = total.astype(jnp.bfloat16)
                    return carry

                lax.fori_loop(0, TPD, finish, 0)
                send_out(2 + s, h, rows)

    sent = CAP * (NHEAD - 1) * HPD
    for a in range(4):
        wait_bytes(k_all[0].at[pl.ds(0, sent)], x_send.at[a])
        wait_bytes(k_all[0].at[pl.ds(0, sent)], y_send.at[a])
        wait_bytes((o_out, dq_out, dk_out, dv_out)[a], y_recv.at[a])
    for s in range(2):
        for h in range(HPD):
            for n, rows in enumerate(PARTS_BACK[s, h]):
                wait_bytes((k_stage, v_stage)[s][h].at[:, pl.ds(*rows)], b_send.at[s, h, n])


def hand_over(*refs):
    copies = [
        pltpu.make_async_copy(refs[a].at[p], refs[4 + a].at[p], refs[8].at[a, p]) for a in range(4) for p in range(2)
    ]
    for copy in copies:
        copy.start()
    for copy in copies:
        copy.wait()


def body(query, key_in, value, out_grad, segment, kv_list):
    tokens, width = query.shape
    shape = (tokens // TILE, TILE, width)
    bf16, f32 = jnp.bfloat16, jnp.float32

    def vmem(n, dtype=bf16, rows=TILE):
        return pltpu.VMEM((n, rows, HEAD_DIM), dtype)

    def vmem_parts(n, parts):
        return [vmem(n, rows=rows) for s in range(2) for h in range(HPD) for _, rows in parts[s, h]]

    scratch = (
        [vmem(TPD)] * (2 * HPD)
        + vmem_parts(TPD, PARTS_IN)
        + vmem_parts(NREM, PARTS_BACK)
        + [vmem(SLOTS)] * (2 * HPD)
        + [vmem(NREM)] * (2 * HPD)
        + [vmem(TPD)] * (4 * HPD)
        + [vmem(TPD, f32)] * (2 * HPD)
        + [vmem(ROWS), vmem(ROWS), vmem(HALF, f32), vmem(HALF), vmem(NREM + 1, f32)]
        + [
            pltpu.VMEM((LIST, NCTX * TPD), jnp.int32),
            pltpu.VMEM((NCTX * TPD, TILE), jnp.int32),
            pltpu.VMEM((T_ROWS, TILE), jnp.int32),
            pltpu.VMEM((8, TILE), jnp.int32),
            pltpu.SMEM((T_ROWS, TILE), jnp.int32),
            pltpu.SMEM((8, TILE), jnp.int32),
            pltpu.SemaphoreType.DMA((4,)),
            pltpu.SemaphoreType.DMA((4,)),
            pltpu.SemaphoreType.DMA((4, HPD, MOST_PARTS)),
            pltpu.SemaphoreType.DMA((2, HPD, MOST_PARTS)),
            pltpu.SemaphoreType.DMA((2, HPD, MOST_PARTS)),
            pltpu.SemaphoreType.DMA((2, HPD, MOST_PARTS)),
            pltpu.SemaphoreType.DMA((2, HPD, MOST_PARTS)),
            pltpu.SemaphoreType.DMA((4,)),
            pltpu.SemaphoreType.DMA((4,)),
        ]
    )
    outs = pl.pallas_call(
        kernel,
        out_shape=[pltpu.VMEM(shape, bf16)] * 4,
        in_specs=[pl.BlockSpec(memory_space=pl.ANY)] * 6,
        out_specs=[pl.BlockSpec(memory_space=pl.ANY)] * 4,
        scratch_shapes=scratch,
        compiler_params=pltpu.CompilerParams(
            collective_id=0, has_side_effects=True, vmem_limit_bytes=52 * 1024 * 1024
        ),
        cost_estimate=pl.CostEstimate(flops=7_250_000_000, bytes_accessed=12_600_000, transcendentals=4_718_592),
        name="sparse_attention",
    )(*(a.reshape(shape) for a in (query, key_in, value, out_grad)), segment.reshape(NCTX * TPD, TILE), kv_list.T)
    outs = pl.pallas_call(
        hand_over,
        out_shape=[jax.ShapeDtypeStruct(shape, bf16)] * 4,
        in_specs=[pl.BlockSpec(memory_space=pl.ANY)] * 4,
        out_specs=[pl.BlockSpec(memory_space=pl.ANY)] * 4,
        scratch_shapes=[pltpu.SemaphoreType.DMA((4, 2))],
        compiler_params=pltpu.CompilerParams(vmem_limit_bytes=4 * 1024 * 1024),
        name="hand_over",
    )(*outs)
    return tuple(o.reshape(tokens, width) for o in outs)


def solution(mesh):
    tokens = P(("ctx", "head"), None)
    return jax.shard_map(
        body,
        mesh=mesh,
        in_specs=(tokens, tokens, tokens, tokens, P(), P()),
        out_specs=(tokens, tokens, tokens, tokens),
        check_vma=False,
    )
```

```python
import jax
import jax.numpy as jnp
from jax import lax
from jax.experimental import pallas as pl
from jax.experimental.pallas import tpu as pltpu
from jax.sharding import PartitionSpec as P

HEAD_DIM = 128
TILE = 128
LIST = 6
CAP = 2
TPD = 16
NCTX = 16
NHEAD = 8
HPD = 3
NREM = (NCTX - 1) * CAP
SLOTS = TPD + NREM
ROWS = TPD * LIST
HALF = ROWS // 2
MASKED = -1e30
SCALE = HEAD_DIM**-0.5
LOG2E = 1.4426950408889634
MESH = pl.DeviceIdType.MESH

OFFSETS = (
    (1, 1), (3, 3), (1, 3), (3, 1), (0, 2), (2, 0), (2, 2), (1, 2), (3, 0), (3, 2), (1, 0), (2, 1), (0, 3), (2, 3), (0, 1),
)

AROUND = ((2, 0), (1, 0), (3, 0), (2, 1), (3, 1), (1, 1), (0, 1))

WHOLE = ((0, TILE),)
HALVES = ((0, 64), (64, 64))
RISING = ((0, 32), (32, 32), (64, 64))
FALLING = ((0, 64), (64, 32), (96, 32))
PARTS_IN = {(s, h): WHOLE for s in range(2) for h in range(HPD)} | {(0, 0): RISING}
PARTS_BACK = {(s, h): HALVES for s in range(2) for h in range(HPD)} | {(0, HPD - 1): HALVES, (1, HPD - 1): FALLING}
MOST_PARTS = 3
LATE = {(1, 1, 1): ((1, 2, 0),), (0, 2, 0): ((1, 2, 1), (1, 2, 2))}

T_SLOT, T_TILE = 0, 1
T_LPERM, T_LSAME, T_LLAST = 3, 4, 5
T_RPERM, T_RSAME, T_RLAST = 6, 7, 8
T_BPERM, T_BSAME, T_BLAST = 9, 10, 11
T_EDGE = 12
T_ROWS = 16


def relative(y, z, other):
    return (((other >> 2) - y) & 3) * 4 + (((other & 3) - z) & 3)


def wanted_tiles(me, kv):
    y, z = me // 4, me % 4
    at = lax.broadcasted_iota(jnp.int32, (TILE, 1), 0)
    wide = lax.broadcasted_iota(jnp.int32, (TILE, NCTX * TPD), 1)
    low = jnp.full((1, NCTX * TPD), TPD, jnp.int32)
    high = jnp.full((1, NCTX * TPD), -1, jnp.int32)
    for j in range(LIST):
        row = kv[j : j + 1, :]
        asked = (row >> 4) == me
        low = jnp.where(asked, jnp.minimum(low, row & 15), low)
        high = jnp.where(asked, jnp.maximum(high, row & 15), high)
    step = (at >> 1) + 1
    asker = ((y + (step >> 2)) & 3) * 4 + ((z + (step & 3)) & 3)
    group = (wide >> 4) == asker
    first = jnp.min(jnp.where(group, low, TPD), axis=1, keepdims=True)
    second = jnp.max(jnp.where(group, high, -1), axis=1, keepdims=True)
    return jnp.clip(jnp.where((at & 1) == 0, first, second), 0, TPD - 1)


def diagonal(col):
    eye = lax.broadcasted_iota(jnp.int32, (TILE, TILE), 0) == lax.broadcasted_iota(jnp.int32, (TILE, TILE), 1)
    return jnp.sum(jnp.where(eye, col, 0), axis=0, keepdims=True)


def build_tables(me, kv, seg, want_r, table):
    y, z = me // 4, me % 4
    big = 1 << 20
    sub = lax.broadcasted_iota(jnp.int32, (TILE, TILE), 0)
    lane = lax.broadcasted_iota(jnp.int32, (TILE, TILE), 1)
    at = lax.broadcasted_iota(jnp.int32, (TILE, 1), 0)

    def count(mask):
        return jnp.sum(jnp.where(mask, 1, 0), axis=0, keepdims=True)

    def runs(key_c, key_r, valid_c, valid_r):
        full_c = jnp.where(valid_c, key_c * TILE + at, big)
        full_r = jnp.where(valid_r, key_r * TILE + lane, big)
        place = jnp.sum(jnp.where(full_r < full_c, 1, 0), axis=1, keepdims=True)
        hit = (place == lane) & valid_c
        after = (place + 1 == lane) & valid_c
        perm = jnp.sum(jnp.where(hit, sub, 0), axis=0, keepdims=True)
        key = jnp.sum(jnp.where(hit, key_c + 1, 0), axis=0, keepdims=True)
        before = jnp.sum(jnp.where(after, key_c + 1, 0), axis=0, keepdims=True)
        return perm, jnp.where(key == before, 1, 0)

    wide = lax.broadcasted_iota(jnp.int32, (TILE, NCTX * TPD), 1)
    rows = [kv[j : j + 1, :] for j in range(LIST)]
    want_c = jnp.sum(jnp.where(sub == lane, want_r, 0), axis=1, keepdims=True)
    mine_c = jnp.zeros((TILE, 1), jnp.int32)
    for j in range(LIST):
        here = (wide == me * TPD + (at & 15)) & ((at >> 4) == j)
        mine_c = mine_c + jnp.sum(jnp.where(here, rows[j], 0), axis=1, keepdims=True)
    mine_r = diagonal(mine_c)
    own_c, own_r = mine_c >> 4, mine_r >> 4
    in_c, in_r = mine_c & 15, mine_r & 15
    real_c, real_r = at < ROWS, lane < ROWS
    lowest = jnp.min(jnp.where((own_c == own_r) & real_r, in_r, TPD), axis=1, keepdims=True)
    rank = jnp.where(in_c != lowest, 1, 0)
    slot_c = jnp.where(own_c == me, in_c, TPD + CAP * (relative(y, z, own_c) - 1) + rank)
    slot_r = diagonal(slot_c)
    local_c, local_r = (own_c == me) & real_c, (own_r == me) & real_r
    other_c, other_r = (own_c != me) & real_c, (own_r != me) & real_r
    l_perm, l_same = runs(slot_c, slot_r, local_c, local_r)
    r_perm, r_same = runs(slot_c, slot_r, other_c, other_r)
    asked_c, asked_r = at < NREM, lane < NREM
    b_perm, b_same = runs(want_c, want_r, asked_c, asked_r)
    upto = count((want_c <= lane) & asked_c)
    b_last = jnp.where(count((want_c == lane) & asked_c) > 0, upto, 0)
    edges = []
    for value in (1, 2):
        per_lane = jnp.sum(jnp.where(seg[...] < value, 1, 0), axis=0, keepdims=True)
        edges.append(jnp.sum(per_lane, axis=1, keepdims=True))
    lane_r = lax.broadcasted_iota(jnp.int32, (1, TILE), 1)
    found = {
        T_SLOT: slot_r,
        T_TILE: mine_r,
        T_LPERM: l_perm,
        T_LSAME: l_same,
        T_LLAST: jnp.clip(count((slot_c <= lane) & local_c) - 1, 0, HALF - 1),
        T_RPERM: r_perm,
        T_RSAME: r_same,
        T_RLAST: jnp.clip(count((slot_c - TPD <= lane) & other_c) - 1, 0, HALF - 1),
        T_BPERM: b_perm,
        T_BSAME: b_same,
        T_BLAST: b_last,
        T_EDGE: jnp.where(lane_r == 0, edges[0], edges[1]),
    }
    none = jnp.zeros((1, TILE), jnp.int32)
    table[...] = jnp.concatenate([found.get(r, none) for r in range(T_ROWS)], axis=0)


def dot_nt(a, b):
    return lax.dot_general(a, b, (((1,), (1,)), ((), ())), preferred_element_type=jnp.float32)


def dot_nn(a, b):
    return lax.dot_general(a, b, (((1,), (0,)), ((), ())), preferred_element_type=jnp.float32)


def dot_tn(a, b):
    return lax.dot_general(a, b, (((0,), (0,)), ((), ())), preferred_element_type=jnp.float32)


def attend(tab, me, q, g, k_all, v_all, o_out, dq_out, c_key, c_value):
    edge1, edge2 = tab[T_EDGE, 0], tab[T_EDGE, 1]
    end = NCTX * TPD * TILE

    def one(i, carry):
        query, grad = q[i], g[i]
        slots = [tab[T_SLOT, j * TPD + i] for j in range(LIST)]
        keys = jnp.concatenate([k_all[s] for s in slots], axis=0)
        values = jnp.concatenate([v_all[s] for s in slots], axis=0)
        scores = dot_nt(query, keys) * (SCALE * LOG2E)
        at = (me * TPD + i) * TILE + lax.broadcasted_iota(jnp.int32, (TILE, TILE), 0)
        start = jnp.where(at >= edge2, edge2, jnp.where(at >= edge1, edge1, 0))
        stop = jnp.where(at >= edge2, end, jnp.where(at >= edge1, edge2, edge1))
        lane = lax.broadcasted_iota(jnp.int32, (TILE, TILE), 1)
        parts = []
        for j in range(LIST):
            key_at = tab[T_TILE, j * TPD + i] * TILE + lane
            allowed = (key_at >= start) & (key_at < stop)
            parts.append(jnp.where(allowed, scores[:, j * TILE : (j + 1) * TILE], MASKED))
        scores = jnp.concatenate(parts, axis=1)
        top = jnp.max(scores, axis=1, keepdims=True)
        expd = jnp.exp2(scores - top)
        probs = expd * (1.0 / jnp.sum(expd, axis=1, keepdims=True))
        low = probs.astype(jnp.bfloat16)
        attended = dot_nn(low, values).astype(jnp.bfloat16)
        o_out[i] = attended
        grad_probs = dot_nt(grad, values)
        row_dot = jnp.sum(grad.astype(jnp.float32) * attended.astype(jnp.float32), axis=1, keepdims=True)
        grad_scores = (probs * (grad_probs - row_dot)).astype(jnp.bfloat16)
        dq_out[i] = (dot_nn(grad_scores, keys) * SCALE).astype(jnp.bfloat16)
        key_part = (dot_tn(grad_scores, query) * SCALE).astype(jnp.bfloat16)
        value_part = dot_tn(low, grad).astype(jnp.bfloat16)
        for j in range(LIST):
            c_key[j * TPD + i] = key_part[j * TILE : (j + 1) * TILE]
            c_value[j * TPD + i] = value_part[j * TILE : (j + 1) * TILE]
        return carry

    lax.fori_loop(0, TPD, one, 0)


def run_sums(tab, perm, same, count, parts, out, shift=0, rows=TILE):
    def one(p, total):
        total = jnp.where(tab[same, p] == 1, total, 0.0) + parts[tab[perm, p]].astype(jnp.float32)
        out[p + shift, pl.ds(0, rows)] = total.astype(out.dtype)
        return total

    lax.fori_loop(0, count, one, jnp.zeros((rows, HEAD_DIM), jnp.float32))


def wait_bytes(ref, sem):
    pltpu.make_async_copy(ref, ref, sem).wait()


def kernel(q_in, k_in, v_in, g_in, seg_in, kv_in, o_out, dq_out, dk_out, dv_out, *scratch):
    it = iter(scratch)

    def take(n):
        return [next(it) for _ in range(n)]

    def take_parts(parts):
        return {(s, h): take(len(parts[s, h])) for s in range(2) for h in range(HPD)}

    q_loc, g_loc = take(HPD), take(HPD)
    kv_loc, kv_back = take_parts(PARTS_IN), take_parts(PARTS_BACK)
    k_all, v_all = take(HPD), take(HPD)
    k_stage, v_stage = take(HPD), take(HPD)
    o_stage, dq_stage, dk_stage, dv_stage = take(HPD), take(HPD), take(HPD), take(HPD)
    k_sum, v_sum = take(HPD), take(HPD)
    c_key, c_value, run_local, run_remote, run_back = take(5)
    kv, seg, table, want_table, tab, want_tab, t_sem = take(7)
    x_send, x_recv, c_send, c_recv, b_send, b_recv, y_send, y_recv = take(8)

    me, head = lax.axis_index("ctx"), lax.axis_index("head")
    y, z, core = me // 4, me % 4, head % 2

    fetches = [pltpu.make_async_copy(kv_in, kv, t_sem.at[0]), pltpu.make_async_copy(seg_in, seg, t_sem.at[1])]
    for fetch in fetches:
        fetch.start()

    barrier = pltpu.get_barrier_semaphore()
    for d in range(1, NHEAD):
        pl.semaphore_signal(barrier, inc=1, device_id=(me, (head + d) % NHEAD), device_id_type=MESH)
    for dy, dz in OFFSETS:
        peer = ((y + dy) % 4) * 4 + (z + dz) % 4
        pl.semaphore_signal(barrier, inc=1, device_id=(peer, head), device_id_type=MESH)
    pl.semaphore_wait(barrier, NHEAD - 1 + NCTX - 1)

    def neighbour(chips, cores):
        along = jnp.where(core == 0, chips, (4 - chips) % 4)
        return ((head // 2 + along) % 4) * 2 + (core + cores) % 2

    def columns(owner, h):
        return pl.ds(pl.multiple_of((owner * HPD + h) * HEAD_DIM, HEAD_DIM), HEAD_DIM)

    def pair(index):
        return pl.ds(2 * index, 2)

    def send_in(src, dst, rows, h, send_sem, recv_sem):
        for chips, cores in AROUND:
            peer = neighbour(chips, cores)
            pltpu.make_async_remote_copy(
                src_ref=src.at[:, pl.ds(*rows), columns(peer, h)],
                dst_ref=dst.at[pair(head)],
                send_sem=send_sem,
                recv_sem=recv_sem,
                device_id=(me, peer),
                device_id_type=MESH,
            ).start()
        pltpu.make_async_copy(src.at[:, pl.ds(*rows), columns(head, h)], dst.at[pair(head)], recv_sem).start()

    def send_kv(s, h, n=0):
        rows = PARTS_IN[s, h][n]
        send_in((k_in, v_in)[s], kv_loc[s, h][n], rows, h, x_send.at[2 + s], x_recv.at[2 + s, h, n])

    def send_qg(h):
        send_in(q_in, q_loc[h], WHOLE[0], h, x_send.at[0], x_recv.at[0, h, 0])
        send_in(g_in, g_loc[h], WHOLE[0], h, x_send.at[1], x_recv.at[1, h, 0])

    def send_out(a, h, rows):
        src, dst = (o_stage, dq_stage, dk_stage, dv_stage)[a][h], (o_out, dq_out, dk_out, dv_out)[a]
        for chips, cores in AROUND:
            peer = neighbour(chips, cores)
            pltpu.make_async_remote_copy(
                src_ref=src.at[pair(peer), pl.ds(*rows)],
                dst_ref=dst.at[:, pl.ds(*rows), columns(head, h)],
                send_sem=y_send.at[a],
                recv_sem=y_recv.at[a],
                device_id=(me, peer),
                device_id_type=MESH,
            ).start()
        pltpu.make_async_copy(
            src.at[pair(head), pl.ds(*rows)], dst.at[:, pl.ds(*rows), columns(head, h)], y_recv.at[a]
        ).start()

    def send_ctx(stage, landing, base, rows, landing_rows, send_sem, recv_sem):
        for one, two in OFFSETS:
            dy, dz = jnp.where(core == 0, one, two), jnp.where(core == 0, two, one)
            there = dy * 4 + dz - 1
            here = ((4 - dy) % 4) * 4 + (4 - dz) % 4 - 1
            peer = ((y + dy) % 4) * 4 + (z + dz) % 4
            pltpu.make_async_remote_copy(
                src_ref=stage.at[pl.ds(CAP * there, CAP), pl.ds(*rows)],
                dst_ref=landing.at[pl.ds(base + CAP * here, CAP), pl.ds(*landing_rows)],
                send_sem=send_sem,
                recv_sem=recv_sem,
                device_id=(peer, head),
                device_id_type=MESH,
            ).start()

    def wait_kv(s, h, n=0):
        wait_bytes(kv_loc[s, h][n], x_recv.at[2 + s, h, n])

    def forward_tiles(s, h, n=0):
        stage, everything = (k_stage, v_stage)[s][h], (k_all, v_all)[s][h]
        rows, local = PARTS_IN[s, h][n], kv_loc[s, h][n]

        def pack(p, carry):
            stage[p, pl.ds(*rows)] = local[want_tab[0, p]]
            return carry

        lax.fori_loop(0, NREM, pack, 0)
        send_ctx(stage, everything, TPD, rows, rows, c_send.at[s, h, n], c_recv.at[s, h, n])

        def keep(p, carry):
            everything[p, pl.ds(*rows)] = local[p]
            return carry

        lax.fori_loop(0, TPD, keep, 0)

    def forward(s, h, n=0):
        wait_kv(s, h, n)
        forward_tiles(s, h, n)

    send_kv(0, 0, 0)
    fetches[0].wait()
    want = diagonal(wanted_tiles(me, kv))
    want_table[...] = jnp.broadcast_to(want, (8, TILE))
    to_scalar = pltpu.make_async_copy(want_table, want_tab, t_sem.at[2])
    to_scalar.start()
    send_kv(0, 0, 1)
    send_kv(0, 0, 2)
    to_scalar.wait()
    send_kv(1, 0)
    forward(0, 0, 0)
    send_kv(0, 1)
    forward(0, 0, 1)
    send_kv(1, 1)
    forward(0, 0, 2)
    send_kv(0, 2)
    forward(1, 0)
    send_kv(1, 2)
    fetches[1].wait()
    build_tables(me, kv, seg, want, table)
    to_scalar = pltpu.make_async_copy(table, tab, t_sem.at[3])
    to_scalar.start()
    forward(0, 1)
    send_qg(0)
    forward(1, 1)
    send_qg(1)
    forward(0, 2)
    send_qg(2)
    forward(1, 2)
    to_scalar.wait()

    def send_back(s, h, n):
        rows, stage, landing = PARTS_BACK[s, h][n], (k_stage, v_stage)[s][h], kv_back[s, h][n]
        send_ctx(stage, landing, 0, rows, (0, rows[1]), b_send.at[s, h, n], b_recv.at[s, h, n])

    for h in range(HPD):
        wait_bytes(q_loc[h], x_recv.at[0, h, 0])
        wait_bytes(g_loc[h], x_recv.at[1, h, 0])
        for s in range(2):
            for n, rows in enumerate(PARTS_IN[s, h]):
                wait_bytes((k_all, v_all)[s][h].at[pl.ds(TPD, NREM), pl.ds(*rows)], c_recv.at[s, h, n])
        attend(tab, me, q_loc[h], g_loc[h], k_all[h], v_all[h], o_stage[h], dq_stage[h], c_key, c_value)
        send_out(0, h, WHOLE[0])
        send_out(1, h, WHOLE[0])
        for s in range(2):
            stage = (k_stage, v_stage)[s][h]
            run_sums(tab, T_RPERM, T_RSAME, HALF, (c_key, c_value)[s], run_remote)
            for n, rows in enumerate(PARTS_IN[s, h]):
                wait_bytes(stage.at[:, pl.ds(*rows)], c_send.at[s, h, n])

            def fill(p, carry, stage=stage):
                stage[p] = run_remote[tab[T_RLAST, p]]
                return carry

            lax.fori_loop(0, NREM, fill, 0)
            for n in range(len(PARTS_BACK[s, h])):
                if (s, h, n) not in sum(LATE.values(), ()):
                    send_back(s, h, n)
        for s in range(2):
            sums = (k_sum, v_sum)[s][h]
            run_sums(tab, T_LPERM, T_LSAME, HALF, (c_key, c_value)[s], run_local)

            def settle(p, carry, sums=sums):
                sums[p] = run_local[tab[T_LLAST, p]]
                return carry

            lax.fori_loop(0, TPD, settle, 0)

    run_back[0] = jnp.zeros((TILE, HEAD_DIM), jnp.float32)
    for h in range(HPD):
        for s in range(2):
            sums, stage = (k_sum, v_sum)[s][h], (dk_stage, dv_stage)[s][h]
            for n, rows in enumerate(PARTS_BACK[s, h]):
                back = kv_back[s, h][n]
                wait_bytes(back, b_recv.at[s, h, n])
                for later in LATE.get((s, h, n), ()):
                    send_back(*later)
                run_sums(tab, T_BPERM, T_BSAME, NREM, back, run_back, shift=1, rows=rows[1])

                def finish(p, carry, sums=sums, stage=stage, rows=rows):
                    total = sums[p, pl.ds(*rows)] + run_back[tab[T_BLAST, p], pl.ds(0, rows[1])]
                    stage[p, pl.ds(*rows)] = total.astype(jnp.bfloat16)
                    return carry

                lax.fori_loop(0, TPD, finish, 0)
                send_out(2 + s, h, rows)

    sent = CAP * (NHEAD - 1) * HPD
    for a in range(4):
        wait_bytes(k_all[0].at[pl.ds(0, sent)], x_send.at[a])
        wait_bytes(k_all[0].at[pl.ds(0, sent)], y_send.at[a])
        wait_bytes((o_out, dq_out, dk_out, dv_out)[a], y_recv.at[a])
    for s in range(2):
        for h in range(HPD):
            for n, rows in enumerate(PARTS_BACK[s, h]):
                wait_bytes((k_stage, v_stage)[s][h].at[:, pl.ds(*rows)], b_send.at[s, h, n])


def hand_over(*refs):
    copies = [
        pltpu.make_async_copy(refs[a].at[p], refs[4 + a].at[p], refs[8].at[a, p]) for a in range(4) for p in range(2)
    ]
    for copy in copies:
        copy.start()
    for copy in copies:
        copy.wait()


def body(query, key_in, value, out_grad, segment, kv_list):
    tokens, width = query.shape
    shape = (tokens // TILE, TILE, width)
    bf16, f32 = jnp.bfloat16, jnp.float32

    def vmem(n, dtype=bf16, rows=TILE):
        return pltpu.VMEM((n, rows, HEAD_DIM), dtype)

    def vmem_parts(n, parts):
        return [vmem(n, rows=rows) for s in range(2) for h in range(HPD) for _, rows in parts[s, h]]

    scratch = (
        [vmem(TPD)] * (2 * HPD)
        + vmem_parts(TPD, PARTS_IN)
        + vmem_parts(NREM, PARTS_BACK)
        + [vmem(SLOTS)] * (2 * HPD)
        + [vmem(NREM)] * (2 * HPD)
        + [vmem(TPD)] * (4 * HPD)
        + [vmem(TPD, f32)] * (2 * HPD)
        + [vmem(ROWS), vmem(ROWS), vmem(HALF, f32), vmem(HALF), vmem(NREM + 1, f32)]
        + [
            pltpu.VMEM((LIST, NCTX * TPD), jnp.int32),
            pltpu.VMEM((NCTX * TPD, TILE), jnp.int32),
            pltpu.VMEM((T_ROWS, TILE), jnp.int32),
            pltpu.VMEM((8, TILE), jnp.int32),
            pltpu.SMEM((T_ROWS, TILE), jnp.int32),
            pltpu.SMEM((8, TILE), jnp.int32),
            pltpu.SemaphoreType.DMA((4,)),
            pltpu.SemaphoreType.DMA((4,)),
            pltpu.SemaphoreType.DMA((4, HPD, MOST_PARTS)),
            pltpu.SemaphoreType.DMA((2, HPD, MOST_PARTS)),
            pltpu.SemaphoreType.DMA((2, HPD, MOST_PARTS)),
            pltpu.SemaphoreType.DMA((2, HPD, MOST_PARTS)),
            pltpu.SemaphoreType.DMA((2, HPD, MOST_PARTS)),
            pltpu.SemaphoreType.DMA((4,)),
            pltpu.SemaphoreType.DMA((4,)),
        ]
    )
    outs = pl.pallas_call(
        kernel,
        out_shape=[pltpu.VMEM(shape, bf16)] * 4,
        in_specs=[pl.BlockSpec(memory_space=pl.ANY)] * 6,
        out_specs=[pl.BlockSpec(memory_space=pl.ANY)] * 4,
        scratch_shapes=scratch,
        compiler_params=pltpu.CompilerParams(
            collective_id=0, has_side_effects=True, vmem_limit_bytes=52 * 1024 * 1024
        ),
        cost_estimate=pl.CostEstimate(flops=7_250_000_000, bytes_accessed=12_600_000, transcendentals=4_718_592),
        name="sparse_attention",
    )(*(a.reshape(shape) for a in (query, key_in, value, out_grad)), segment.reshape(NCTX * TPD, TILE), kv_list.T)
    outs = pl.pallas_call(
        hand_over,
        out_shape=[jax.ShapeDtypeStruct(shape, bf16)] * 4,
        in_specs=[pl.BlockSpec(memory_space=pl.ANY)] * 4,
        out_specs=[pl.BlockSpec(memory_space=pl.ANY)] * 4,
        scratch_shapes=[pltpu.SemaphoreType.DMA((4, 2))],
        compiler_params=pltpu.CompilerParams(vmem_limit_bytes=4 * 1024 * 1024),
        name="hand_over",
    )(*outs)
    return tuple(o.reshape(tokens, width) for o in outs)


def solution(mesh):
    tokens = P(("ctx", "head"), None)
    return jax.shard_map(
        body,
        mesh=mesh,
        in_specs=(tokens, tokens, tokens, tokens, P(), P()),
        out_specs=(tokens, tokens, tokens, tokens),
        check_vma=False,
    )
```

```python
import jax
import jax.numpy as jnp
from jax import lax
from jax.experimental import pallas as pl
from jax.experimental.pallas import tpu as pltpu
from jax.sharding import PartitionSpec as P

HEAD_DIM = 128
TILE = 128
LIST = 6
CAP = 2
TPD = 16
NCTX = 16
NHEAD = 8
HPD = 3
NREM = (NCTX - 1) * CAP
SLOTS = TPD + NREM
ROWS = TPD * LIST
HALF = ROWS // 2
MASKED = -1e30
SCALE = HEAD_DIM**-0.5
LOG2E = 1.4426950408889634
MESH = pl.DeviceIdType.MESH

OFFSETS = (
    (1, 1), (3, 3), (1, 3), (3, 1), (0, 2), (2, 0), (2, 2), (1, 2), (3, 0), (3, 2), (1, 0), (2, 1), (0, 3), (2, 3), (0, 1),
)

AROUND = ((2, 0), (1, 0), (3, 0), (2, 1), (3, 1), (1, 1), (0, 1))

WHOLE = ((0, TILE),)
HALVES = ((0, 64), (64, 64))
RISING = ((0, 32), (32, 32), (64, 64))
FALLING = ((0, 64), (64, 32), (96, 32))
PARTS_IN = {(s, h): WHOLE for s in range(2) for h in range(HPD)} | {(0, 0): RISING}
PARTS_BACK = {(s, h): HALVES for s in range(2) for h in range(HPD)} | {(0, HPD - 1): HALVES, (1, HPD - 1): FALLING}
MOST_PARTS = 3
LATE = {(1, 1, 1): ((1, 2, 0),), (0, 2, 0): ((1, 2, 1), (1, 2, 2))}

T_SLOT, T_TILE = 0, 1
T_LPERM, T_LSAME, T_LLAST = 3, 4, 5
T_RPERM, T_RSAME, T_RLAST = 6, 7, 8
T_BPERM, T_BSAME, T_BLAST = 9, 10, 11
T_EDGE = 12
T_ROWS = 16


def relative(y, z, other):
    return (((other >> 2) - y) & 3) * 4 + (((other & 3) - z) & 3)


def wanted_tiles(me, kv):
    y, z = me // 4, me % 4
    at = lax.broadcasted_iota(jnp.int32, (TILE, 1), 0)
    wide = lax.broadcasted_iota(jnp.int32, (TILE, NCTX * TPD), 1)
    low = jnp.full((1, NCTX * TPD), TPD, jnp.int32)
    high = jnp.full((1, NCTX * TPD), -1, jnp.int32)
    for j in range(LIST):
        row = kv[j : j + 1, :]
        asked = (row >> 4) == me
        low = jnp.where(asked, jnp.minimum(low, row & 15), low)
        high = jnp.where(asked, jnp.maximum(high, row & 15), high)
    step = (at >> 1) + 1
    asker = ((y + (step >> 2)) & 3) * 4 + ((z + (step & 3)) & 3)
    group = (wide >> 4) == asker
    first = jnp.min(jnp.where(group, low, TPD), axis=1, keepdims=True)
    second = jnp.max(jnp.where(group, high, -1), axis=1, keepdims=True)
    return jnp.clip(jnp.where((at & 1) == 0, first, second), 0, TPD - 1)


def diagonal(col):
    eye = lax.broadcasted_iota(jnp.int32, (TILE, TILE), 0) == lax.broadcasted_iota(jnp.int32, (TILE, TILE), 1)
    return jnp.sum(jnp.where(eye, col, 0), axis=0, keepdims=True)


def build_tables(me, kv, seg, want_r, table):
    y, z = me // 4, me % 4
    big = 1 << 20
    sub = lax.broadcasted_iota(jnp.int32, (TILE, TILE), 0)
    lane = lax.broadcasted_iota(jnp.int32, (TILE, TILE), 1)
    at = lax.broadcasted_iota(jnp.int32, (TILE, 1), 0)

    def count(mask):
        return jnp.sum(jnp.where(mask, 1, 0), axis=0, keepdims=True)

    def runs(key_c, key_r, valid_c, valid_r):
        full_c = jnp.where(valid_c, key_c * TILE + at, big)
        full_r = jnp.where(valid_r, key_r * TILE + lane, big)
        place = jnp.sum(jnp.where(full_r < full_c, 1, 0), axis=1, keepdims=True)
        hit = (place == lane) & valid_c
        after = (place + 1 == lane) & valid_c
        perm = jnp.sum(jnp.where(hit, sub, 0), axis=0, keepdims=True)
        key = jnp.sum(jnp.where(hit, key_c + 1, 0), axis=0, keepdims=True)
        before = jnp.sum(jnp.where(after, key_c + 1, 0), axis=0, keepdims=True)
        return perm, jnp.where(key == before, 1, 0)

    wide = lax.broadcasted_iota(jnp.int32, (TILE, NCTX * TPD), 1)
    rows = [kv[j : j + 1, :] for j in range(LIST)]
    want_c = jnp.sum(jnp.where(sub == lane, want_r, 0), axis=1, keepdims=True)
    mine_c = jnp.zeros((TILE, 1), jnp.int32)
    for j in range(LIST):
        here = (wide == me * TPD + (at & 15)) & ((at >> 4) == j)
        mine_c = mine_c + jnp.sum(jnp.where(here, rows[j], 0), axis=1, keepdims=True)
    mine_r = diagonal(mine_c)
    own_c, own_r = mine_c >> 4, mine_r >> 4
    in_c, in_r = mine_c & 15, mine_r & 15
    real_c, real_r = at < ROWS, lane < ROWS
    lowest = jnp.min(jnp.where((own_c == own_r) & real_r, in_r, TPD), axis=1, keepdims=True)
    rank = jnp.where(in_c != lowest, 1, 0)
    slot_c = jnp.where(own_c == me, in_c, TPD + CAP * (relative(y, z, own_c) - 1) + rank)
    slot_r = diagonal(slot_c)
    local_c, local_r = (own_c == me) & real_c, (own_r == me) & real_r
    other_c, other_r = (own_c != me) & real_c, (own_r != me) & real_r
    l_perm, l_same = runs(slot_c, slot_r, local_c, local_r)
    r_perm, r_same = runs(slot_c, slot_r, other_c, other_r)
    asked_c, asked_r = at < NREM, lane < NREM
    b_perm, b_same = runs(want_c, want_r, asked_c, asked_r)
    upto = count((want_c <= lane) & asked_c)
    b_last = jnp.where(count((want_c == lane) & asked_c) > 0, upto, 0)
    edges = []
    for value in (1, 2):
        per_lane = jnp.sum(jnp.where(seg[...] < value, 1, 0), axis=0, keepdims=True)
        edges.append(jnp.sum(per_lane, axis=1, keepdims=True))
    lane_r = lax.broadcasted_iota(jnp.int32, (1, TILE), 1)
    found = {
        T_SLOT: slot_r,
        T_TILE: mine_r,
        T_LPERM: l_perm,
        T_LSAME: l_same,
        T_LLAST: jnp.clip(count((slot_c <= lane) & local_c) - 1, 0, HALF - 1),
        T_RPERM: r_perm,
        T_RSAME: r_same,
        T_RLAST: jnp.clip(count((slot_c - TPD <= lane) & other_c) - 1, 0, HALF - 1),
        T_BPERM: b_perm,
        T_BSAME: b_same,
        T_BLAST: b_last,
        T_EDGE: jnp.where(lane_r == 0, edges[0], edges[1]),
    }
    none = jnp.zeros((1, TILE), jnp.int32)
    table[...] = jnp.concatenate([found.get(r, none) for r in range(T_ROWS)], axis=0)


def dot_nt(a, b):
    return lax.dot_general(a, b, (((1,), (1,)), ((), ())), preferred_element_type=jnp.float32)


def dot_nn(a, b):
    return lax.dot_general(a, b, (((1,), (0,)), ((), ())), preferred_element_type=jnp.float32)


def dot_tn(a, b):
    return lax.dot_general(a, b, (((0,), (0,)), ((), ())), preferred_element_type=jnp.float32)


def attend(tab, me, q, g, k_all, v_all, o_out, dq_out, c_key, c_value):
    edge1, edge2 = tab[T_EDGE, 0], tab[T_EDGE, 1]
    end = NCTX * TPD * TILE

    def one(i, carry):
        query, grad = q[i], g[i]
        slots = [tab[T_SLOT, j * TPD + i] for j in range(LIST)]
        keys = jnp.concatenate([k_all[s] for s in slots], axis=0)
        values = jnp.concatenate([v_all[s] for s in slots], axis=0)
        scores = dot_nt(query, keys) * (SCALE * LOG2E)
        at = (me * TPD + i) * TILE + lax.broadcasted_iota(jnp.int32, (TILE, TILE), 0)
        start = jnp.where(at >= edge2, edge2, jnp.where(at >= edge1, edge1, 0))
        stop = jnp.where(at >= edge2, end, jnp.where(at >= edge1, edge2, edge1))
        lane = lax.broadcasted_iota(jnp.int32, (TILE, TILE), 1)
        parts = []
        for j in range(LIST):
            key_at = tab[T_TILE, j * TPD + i] * TILE + lane
            allowed = (key_at >= start) & (key_at < stop)
            parts.append(jnp.where(allowed, scores[:, j * TILE : (j + 1) * TILE], MASKED))
        scores = jnp.concatenate(parts, axis=1)
        top = jnp.max(scores, axis=1, keepdims=True)
        expd = jnp.exp2(scores - top)
        probs = expd * (1.0 / jnp.sum(expd, axis=1, keepdims=True))
        low = probs.astype(jnp.bfloat16)
        attended = dot_nn(low, values).astype(jnp.bfloat16)
        o_out[i] = attended
        grad_probs = dot_nt(grad, values)
        row_dot = jnp.sum(grad.astype(jnp.float32) * attended.astype(jnp.float32), axis=1, keepdims=True)
        grad_scores = (probs * (grad_probs - row_dot)).astype(jnp.bfloat16)
        dq_out[i] = (dot_nn(grad_scores, keys) * SCALE).astype(jnp.bfloat16)
        key_part = (dot_tn(grad_scores, query) * SCALE).astype(jnp.bfloat16)
        value_part = dot_tn(low, grad).astype(jnp.bfloat16)
        for j in range(LIST):
            c_key[j * TPD + i] = key_part[j * TILE : (j + 1) * TILE]
            c_value[j * TPD + i] = value_part[j * TILE : (j + 1) * TILE]
        return carry

    lax.fori_loop(0, TPD, one, 0)


def run_sums(tab, perm, same, count, parts, out, shift=0, rows=TILE):
    def one(p, total):
        total = jnp.where(tab[same, p] == 1, total, 0.0) + parts[tab[perm, p]].astype(jnp.float32)
        out[p + shift, pl.ds(0, rows)] = total.astype(out.dtype)
        return total

    lax.fori_loop(0, count, one, jnp.zeros((rows, HEAD_DIM), jnp.float32))


def wait_bytes(ref, sem):
    pltpu.make_async_copy(ref, ref, sem).wait()


def kernel(q_in, k_in, v_in, g_in, seg_in, kv_in, o_out, dq_out, dk_out, dv_out, *scratch):
    it = iter(scratch)

    def take(n):
        return [next(it) for _ in range(n)]

    def take_parts(parts):
        return {(s, h): take(len(parts[s, h])) for s in range(2) for h in range(HPD)}

    q_loc, g_loc = take(HPD), take(HPD)
    kv_loc, kv_back = take_parts(PARTS_IN), take_parts(PARTS_BACK)
    k_all, v_all = take(HPD), take(HPD)
    k_stage, v_stage = take(HPD), take(HPD)
    o_stage, dq_stage, dk_stage, dv_stage = take(HPD), take(HPD), take(HPD), take(HPD)
    k_sum, v_sum = take(HPD), take(HPD)
    c_key, c_value, run_local, run_remote, run_back = take(5)
    kv, seg, table, want_table, tab, want_tab, t_sem = take(7)
    x_send, x_recv, c_send, c_recv, b_send, b_recv, y_send, y_recv = take(8)

    me, head = lax.axis_index("ctx"), lax.axis_index("head")
    y, z, core = me // 4, me % 4, head % 2

    fetches = [pltpu.make_async_copy(kv_in, kv, t_sem.at[0]), pltpu.make_async_copy(seg_in, seg, t_sem.at[1])]
    for fetch in fetches:
        fetch.start()

    barrier = pltpu.get_barrier_semaphore()
    for d in range(1, NHEAD):
        pl.semaphore_signal(barrier, inc=1, device_id=(me, (head + d) % NHEAD), device_id_type=MESH)
    for dy, dz in OFFSETS:
        peer = ((y + dy) % 4) * 4 + (z + dz) % 4
        pl.semaphore_signal(barrier, inc=1, device_id=(peer, head), device_id_type=MESH)
    pl.semaphore_wait(barrier, NHEAD - 1 + NCTX - 1)

    def neighbour(chips, cores):
        along = jnp.where(core == 0, chips, (4 - chips) % 4)
        return ((head // 2 + along) % 4) * 2 + (core + cores) % 2

    def columns(owner, h):
        return pl.ds(pl.multiple_of((owner * HPD + h) * HEAD_DIM, HEAD_DIM), HEAD_DIM)

    def pair(index):
        return pl.ds(2 * index, 2)

    def send_in(src, dst, rows, h, send_sem, recv_sem):
        for chips, cores in AROUND:
            peer = neighbour(chips, cores)
            pltpu.make_async_remote_copy(
                src_ref=src.at[:, pl.ds(*rows), columns(peer, h)],
                dst_ref=dst.at[pair(head)],
                send_sem=send_sem,
                recv_sem=recv_sem,
                device_id=(me, peer),
                device_id_type=MESH,
            ).start()
        pltpu.make_async_copy(src.at[:, pl.ds(*rows), columns(head, h)], dst.at[pair(head)], recv_sem).start()

    def send_kv(s, h, n=0):
        rows = PARTS_IN[s, h][n]
        send_in((k_in, v_in)[s], kv_loc[s, h][n], rows, h, x_send.at[2 + s], x_recv.at[2 + s, h, n])

    def send_qg(h):
        send_in(q_in, q_loc[h], WHOLE[0], h, x_send.at[0], x_recv.at[0, h, 0])
        send_in(g_in, g_loc[h], WHOLE[0], h, x_send.at[1], x_recv.at[1, h, 0])

    def send_out(a, h, rows):
        src, dst = (o_stage, dq_stage, dk_stage, dv_stage)[a][h], (o_out, dq_out, dk_out, dv_out)[a]
        for chips, cores in AROUND:
            peer = neighbour(chips, cores)
            pltpu.make_async_remote_copy(
                src_ref=src.at[pair(peer), pl.ds(*rows)],
                dst_ref=dst.at[:, pl.ds(*rows), columns(head, h)],
                send_sem=y_send.at[a],
                recv_sem=y_recv.at[a],
                device_id=(me, peer),
                device_id_type=MESH,
            ).start()
        pltpu.make_async_copy(
            src.at[pair(head), pl.ds(*rows)], dst.at[:, pl.ds(*rows), columns(head, h)], y_recv.at[a]
        ).start()

    def send_ctx(stage, landing, base, rows, landing_rows, send_sem, recv_sem):
        for one, two in OFFSETS:
            dy, dz = jnp.where(core == 0, one, two), jnp.where(core == 0, two, one)
            there = dy * 4 + dz - 1
            here = ((4 - dy) % 4) * 4 + (4 - dz) % 4 - 1
            peer = ((y + dy) % 4) * 4 + (z + dz) % 4
            pltpu.make_async_remote_copy(
                src_ref=stage.at[pl.ds(CAP * there, CAP), pl.ds(*rows)],
                dst_ref=landing.at[pl.ds(base + CAP * here, CAP), pl.ds(*landing_rows)],
                send_sem=send_sem,
                recv_sem=recv_sem,
                device_id=(peer, head),
                device_id_type=MESH,
            ).start()

    def wait_kv(s, h, n=0):
        wait_bytes(kv_loc[s, h][n], x_recv.at[2 + s, h, n])

    def forward_tiles(s, h, n=0):
        stage, everything = (k_stage, v_stage)[s][h], (k_all, v_all)[s][h]
        rows, local = PARTS_IN[s, h][n], kv_loc[s, h][n]

        def pack(p, carry):
            stage[p, pl.ds(*rows)] = local[want_tab[0, p]]
            return carry

        lax.fori_loop(0, NREM, pack, 0)
        send_ctx(stage, everything, TPD, rows, rows, c_send.at[s, h, n], c_recv.at[s, h, n])

        def keep(p, carry):
            everything[p, pl.ds(*rows)] = local[p]
            return carry

        lax.fori_loop(0, TPD, keep, 0)

    def forward(s, h, n=0):
        wait_kv(s, h, n)
        forward_tiles(s, h, n)

    send_kv(0, 0, 0)
    fetches[0].wait()
    want = diagonal(wanted_tiles(me, kv))
    want_table[...] = jnp.broadcast_to(want, (8, TILE))
    to_scalar = pltpu.make_async_copy(want_table, want_tab, t_sem.at[2])
    to_scalar.start()
    send_kv(0, 0, 1)
    send_kv(0, 0, 2)
    send_kv(1, 0)
    send_kv(0, 1)
    to_scalar.wait()
    forward(0, 0, 0)
    send_kv(1, 1)
    send_kv(0, 2)
    forward(0, 0, 1)
    send_kv(1, 2)
    send_qg(0)
    forward(0, 0, 2)
    send_qg(1)
    send_qg(2)
    forward(1, 0)
    fetches[1].wait()
    build_tables(me, kv, seg, want, table)
    to_scalar = pltpu.make_async_copy(table, tab, t_sem.at[3])
    to_scalar.start()
    forward(0, 1)
    forward(1, 1)
    forward(0, 2)
    forward(1, 2)
    to_scalar.wait()

    def send_back(s, h, n):
        rows, stage, landing = PARTS_BACK[s, h][n], (k_stage, v_stage)[s][h], kv_back[s, h][n]
        send_ctx(stage, landing, 0, rows, (0, rows[1]), b_send.at[s, h, n], b_recv.at[s, h, n])

    for h in range(HPD):
        wait_bytes(q_loc[h], x_recv.at[0, h, 0])
        wait_bytes(g_loc[h], x_recv.at[1, h, 0])
        for s in range(2):
            for n, rows in enumerate(PARTS_IN[s, h]):
                wait_bytes((k_all, v_all)[s][h].at[pl.ds(TPD, NREM), pl.ds(*rows)], c_recv.at[s, h, n])
        attend(tab, me, q_loc[h], g_loc[h], k_all[h], v_all[h], o_stage[h], dq_stage[h], c_key, c_value)
        send_out(0, h, WHOLE[0])
        send_out(1, h, WHOLE[0])
        for s in range(2):
            stage = (k_stage, v_stage)[s][h]
            run_sums(tab, T_RPERM, T_RSAME, HALF, (c_key, c_value)[s], run_remote)
            for n, rows in enumerate(PARTS_IN[s, h]):
                wait_bytes(stage.at[:, pl.ds(*rows)], c_send.at[s, h, n])

            def fill(p, carry, stage=stage):
                stage[p] = run_remote[tab[T_RLAST, p]]
                return carry

            lax.fori_loop(0, NREM, fill, 0)
            for n in range(len(PARTS_BACK[s, h])):
                if (s, h, n) not in sum(LATE.values(), ()):
                    send_back(s, h, n)
        for s in range(2):
            sums = (k_sum, v_sum)[s][h]
            run_sums(tab, T_LPERM, T_LSAME, HALF, (c_key, c_value)[s], run_local)

            def settle(p, carry, sums=sums):
                sums[p] = run_local[tab[T_LLAST, p]]
                return carry

            lax.fori_loop(0, TPD, settle, 0)

    run_back[0] = jnp.zeros((TILE, HEAD_DIM), jnp.float32)
    for h in range(HPD):
        for s in range(2):
            sums, stage = (k_sum, v_sum)[s][h], (dk_stage, dv_stage)[s][h]
            for n, rows in enumerate(PARTS_BACK[s, h]):
                back = kv_back[s, h][n]
                wait_bytes(back, b_recv.at[s, h, n])
                for later in LATE.get((s, h, n), ()):
                    send_back(*later)
                run_sums(tab, T_BPERM, T_BSAME, NREM, back, run_back, shift=1, rows=rows[1])

                def finish(p, carry, sums=sums, stage=stage, rows=rows):
                    total = sums[p, pl.ds(*rows)] + run_back[tab[T_BLAST, p], pl.ds(0, rows[1])]
                    stage[p, pl.ds(*rows)] = total.astype(jnp.bfloat16)
                    return carry

                lax.fori_loop(0, TPD, finish, 0)
                send_out(2 + s, h, rows)

    sent = CAP * (NHEAD - 1) * HPD
    for a in range(4):
        wait_bytes(k_all[0].at[pl.ds(0, sent)], x_send.at[a])
        wait_bytes(k_all[0].at[pl.ds(0, sent)], y_send.at[a])
        wait_bytes((o_out, dq_out, dk_out, dv_out)[a], y_recv.at[a])
    for s in range(2):
        for h in range(HPD):
            for n, rows in enumerate(PARTS_BACK[s, h]):
                wait_bytes((k_stage, v_stage)[s][h].at[:, pl.ds(*rows)], b_send.at[s, h, n])


def hand_over(*refs):
    copies = [
        pltpu.make_async_copy(refs[a].at[p], refs[4 + a].at[p], refs[8].at[a, p]) for a in range(4) for p in range(2)
    ]
    for copy in copies:
        copy.start()
    for copy in copies:
        copy.wait()


def body(query, key_in, value, out_grad, segment, kv_list):
    tokens, width = query.shape
    shape = (tokens // TILE, TILE, width)
    bf16, f32 = jnp.bfloat16, jnp.float32

    def vmem(n, dtype=bf16, rows=TILE):
        return pltpu.VMEM((n, rows, HEAD_DIM), dtype)

    def vmem_parts(n, parts):
        return [vmem(n, rows=rows) for s in range(2) for h in range(HPD) for _, rows in parts[s, h]]

    scratch = (
        [vmem(TPD)] * (2 * HPD)
        + vmem_parts(TPD, PARTS_IN)
        + vmem_parts(NREM, PARTS_BACK)
        + [vmem(SLOTS)] * (2 * HPD)
        + [vmem(NREM)] * (2 * HPD)
        + [vmem(TPD)] * (4 * HPD)
        + [vmem(TPD, f32)] * (2 * HPD)
        + [vmem(ROWS), vmem(ROWS), vmem(HALF, f32), vmem(HALF), vmem(NREM + 1, f32)]
        + [
            pltpu.VMEM((LIST, NCTX * TPD), jnp.int32),
            pltpu.VMEM((NCTX * TPD, TILE), jnp.int32),
            pltpu.VMEM((T_ROWS, TILE), jnp.int32),
            pltpu.VMEM((8, TILE), jnp.int32),
            pltpu.SMEM((T_ROWS, TILE), jnp.int32),
            pltpu.SMEM((8, TILE), jnp.int32),
            pltpu.SemaphoreType.DMA((4,)),
            pltpu.SemaphoreType.DMA((4,)),
            pltpu.SemaphoreType.DMA((4, HPD, MOST_PARTS)),
            pltpu.SemaphoreType.DMA((2, HPD, MOST_PARTS)),
            pltpu.SemaphoreType.DMA((2, HPD, MOST_PARTS)),
            pltpu.SemaphoreType.DMA((2, HPD, MOST_PARTS)),
            pltpu.SemaphoreType.DMA((2, HPD, MOST_PARTS)),
            pltpu.SemaphoreType.DMA((4,)),
            pltpu.SemaphoreType.DMA((4,)),
        ]
    )
    outs = pl.pallas_call(
        kernel,
        out_shape=[pltpu.VMEM(shape, bf16)] * 4,
        in_specs=[pl.BlockSpec(memory_space=pl.ANY)] * 6,
        out_specs=[pl.BlockSpec(memory_space=pl.ANY)] * 4,
        scratch_shapes=scratch,
        compiler_params=pltpu.CompilerParams(
            collective_id=0, has_side_effects=True, vmem_limit_bytes=52 * 1024 * 1024
        ),
        cost_estimate=pl.CostEstimate(flops=7_250_000_000, bytes_accessed=12_600_000, transcendentals=4_718_592),
        name="sparse_attention",
    )(*(a.reshape(shape) for a in (query, key_in, value, out_grad)), segment.reshape(NCTX * TPD, TILE), kv_list.T)
    outs = pl.pallas_call(
        hand_over,
        out_shape=[jax.ShapeDtypeStruct(shape, bf16)] * 4,
        in_specs=[pl.BlockSpec(memory_space=pl.ANY)] * 4,
        out_specs=[pl.BlockSpec(memory_space=pl.ANY)] * 4,
        scratch_shapes=[pltpu.SemaphoreType.DMA((4, 2))],
        compiler_params=pltpu.CompilerParams(vmem_limit_bytes=4 * 1024 * 1024),
        name="hand_over",
    )(*outs)
    return tuple(o.reshape(tokens, width) for o in outs)


def solution(mesh):
    tokens = P(("ctx", "head"), None)
    return jax.shard_map(
        body,
        mesh=mesh,
        in_specs=(tokens, tokens, tokens, tokens, P(), P()),
        out_specs=(tokens, tokens, tokens, tokens),
        check_vma=False,
    )
```
